128 devices in a mesh: ctx: 64 (over z_lo, x, y, core), ch: 2 (over z_hi).
Axes of the slice: x: 4, y: 4, z: 4 (z_hi: 2, z_lo: 2; z = z_hi * 2 + z_lo), core: 2. Of those that a mesh axis runs over, the one named last changes fastest.
Arguments:
- q_proj: bfloat16 [8192, 4096], P('ctx', 'ch'), may hold values from -6 to 6
- k_proj: bfloat16 [8192, 4096], P('ctx', 'ch'), may hold values from -6 to 6
- v_proj: bfloat16 [8192, 4096], P('ctx', 'ch'), may hold values from -6 to 6
- filt: float32 [256, 256], P(None, 'ch'), may hold values from -3 to 3
- skip: float32 [4096], P('ch'), may hold values from 0.5 to 1.5
- grad_out: bfloat16 [8192, 4096], P('ctx', 'ch'), may hold values from -6 to 6
Outputs:
- mixed_out: bfloat16 [8192, 4096], P('ctx', 'ch')
- q_grad: bfloat16 [8192, 4096], P('ctx', 'ch')
- k_grad: bfloat16 [8192, 4096], P('ctx', 'ch')
- v_grad: bfloat16 [8192, 4096], P('ctx', 'ch')
- filt_grad: float32 [256, 256], P('ctx')
The draws below stay inside these ranges and needn't reach their ends.
All inputs are finite; a program needn't handle non-finite values.
Results may differ from the reference program's by a relative error of at most 0.0054.
Values may be sent and summed in bfloat16 or wider, within the bound.
A program may use at most 192 MiB of HBM per device.

```python
import jax
import jax.numpy as jnp
from jax import lax

C = 4096
GROUP = 16
G = 256
TOKENS = 8192
FLEN = 256


def draw_filt(key, part):
    key = jax.random.fold_in(key, 11)
    key_rate, key_rough, key_amp = jax.random.split(key, 3)
    taps_pos = jnp.arange(FLEN).astype(jnp.float32)[:, None]
    tau = jnp.exp(jax.random.uniform(key_rate, (1, G), jnp.float32, jnp.log(30.0), jnp.log(FLEN * 3.0)))
    rough = jnp.clip(jax.random.normal(key_rough, (FLEN, G), jnp.float32), -4.0, 4.0)
    amp = jnp.sqrt(2.0 / tau) * jnp.exp(jax.random.uniform(key_amp, (1, G), jnp.float32, jnp.log(0.5), jnp.log(2.0)))
    return amp * jnp.exp(-taps_pos / tau) * rough


def block_levels(own_key, dims, pieces, low, top_value):
    def one(position, parts):
        heights = jax.random.uniform(jax.random.fold_in(jax.random.fold_in(own_key, 6), position), (parts,), jnp.float32, low / len(pieces), top_value / len(pieces))
        return jnp.repeat(jnp.exp(heights), dims[position] // parts).reshape((-1,) + (1,) * (len(dims) - position - 1))

    level = one(*pieces[0])
    for cut in pieces[1:]:
        level = level * one(*cut)
    return level


def gaussian(key, dims, spread, limit, cuts=(), kind=jnp.bfloat16):
    gain = block_levels(key, dims, cuts, -0.22, 0.18) if cuts else 1.0
    values = jax.random.normal(key, dims, jnp.float32) * spread * gain
    return jnp.minimum(jnp.maximum(values, -limit), limit).astype(kind)


def setup_inputs(seed: int = 0) -> dict:
    key_list = jax.random.split(jax.random.key(seed), 7)
    return {
        "q_proj": gaussian(key_list[0], (TOKENS, C), 1.0, 6.0, ((0, 64), (1, 2))),
        "k_proj": gaussian(key_list[1], (TOKENS, C), 1.0, 6.0, ((0, 64), (1, 2))),
        "v_proj": gaussian(key_list[2], (TOKENS, C), 1.0, 6.0, ((0, 64), (1, 2))),
        "filt": draw_filt(jax.random.fold_in(key_list[6], 71), 0),
        "skip": jnp.clip(0.5 + 1.0 * jax.random.uniform(key_list[4], (C,), jnp.float32) ** block_levels(key_list[4], (C,), ((0, 2),), -0.2, 0.2), 0.5, 1.5),
        "grad_out": gaussian(key_list[5], (TOKENS, C), 1.0, 6.0, ((0, 64), (1, 2))),
    }


def long_conv(taps_group, stream):
    full_taps = jnp.repeat(taps_group, GROUP, axis=1)
    length = 2 * TOKENS
    width = min(C, 512)
    count = C // width
    taps_blocks = full_taps.reshape(FLEN, count, width).transpose(1, 0, 2)
    stream_blocks = stream.reshape(TOKENS, count, width).transpose(1, 0, 2)

    def one_block(pair):
        taps_piece, stream_piece = pair
        spectrum = jnp.fft.rfft(stream_piece, length, axis=0) * jnp.fft.rfft(taps_piece, length, axis=0)
        return jnp.fft.irfft(spectrum, length, axis=0)[:TOKENS]
    result = lax.map(one_block, (taps_blocks, stream_blocks))
    return result.transpose(1, 0, 2).reshape(TOKENS, C)

def reference(q_proj, k_proj, v_proj, filt, skip, grad_out):
    qf = q_proj.astype(jnp.float32)
    kf = k_proj.astype(jnp.float32)
    vf = v_proj.astype(jnp.float32)
    gf = grad_out.astype(jnp.float32)
    taps = lax.optimization_barrier(filt.astype(jnp.bfloat16)).astype(jnp.float32)
    stream = lax.optimization_barrier((kf * vf).astype(jnp.bfloat16)).astype(jnp.float32)
    conv, pullback = jax.vjp(long_conv, taps, stream)
    conv = conv + skip[None, :] * stream
    mixed_out = (qf * conv).astype(jnp.bfloat16)
    dconv = lax.optimization_barrier((gf * qf).astype(jnp.bfloat16)).astype(jnp.float32)
    q_grad = (gf * conv).astype(jnp.bfloat16)
    taps_grad, dstream = pullback(dconv)
    dstream = dstream + skip[None, :] * dconv
    k_grad = (dstream * vf).astype(jnp.bfloat16)
    v_grad = (dstream * kf).astype(jnp.bfloat16)
    filt_grad = taps_grad / jnp.sqrt(jnp.float32(GROUP * TOKENS))
    return (mixed_out, q_grad, k_grad, v_grad, filt_grad)
```

```python
import functools

import jax
import jax.numpy as jnp
from jax import lax
from jax.experimental import pallas as pl
from jax.experimental.pallas import tpu as pltpu
from jax.sharding import PartitionSpec as P

MESH = pl.DeviceIdType.MESH
F32 = jnp.float32
BF16 = jnp.bfloat16
ROWS = 128
LANES = 2048
TILES = LANES // 128
CHUNKS = 4
PER = TILES // CHUNKS
BLK = 16
NB = ROWS // BLK
TAPS = 256
SPAN = TAPS // BLK + 1
SLOTS = SPAN + 2 * (NB - 1)


def iota(shape, dim):
    return lax.broadcasted_iota(jnp.int32, shape, dim)


def lane_slice(tile, width=128):
    return pl.ds(pl.multiple_of(tile * 128, 128), width)


def kernel(
    n_ctx, scale,
    q_hbm, k_hbm, v_hbm, filt_ref, skip_ref, g_hbm,
    mo_hbm, qg_hbm, kg_hbm, vg_hbm, fg_ref,
    q_ref, k_ref, v_ref, g_ref,
    x_ref, dc_ref, s_ref, o_ref, mask_ref, sh_ref,
    d_ref, d1_ref, r1_ref, a1_ref, r2_ref,
    mo_ref, qg_ref, kg_ref, vg_ref,
    in_sem, out_sem, far_send, far_recv, near_send, near_recv,
    s1_send, s1_recv, s2_send, s2_recv, self_sem,
):
    d = lax.axis_index("ctx")
    h = lax.axis_index("ch")
    up = lax.rem(d + 2, n_ctx)
    down = lax.rem(d + n_ctx - 2, n_ctx)
    core = lax.rem(d, 2)
    mate = d + 1 - 2 * core
    zx = lax.div(d, 8)
    j = lax.rem(d, 8)
    y = lax.div(j, 2)
    n_zx = n_ctx // 8
    n_q = n_zx // 2
    base = zx * 8
    to_self = lax.rem(zx, 2) == core

    ins = []
    for c in range(CHUNKS):
        cols = pl.ds(c * PER * 128, PER * 128)
        row = []
        for n, (src, dst) in enumerate(((k_hbm, k_ref), (v_hbm, v_ref), (g_hbm, g_ref), (q_hbm, q_ref))):
            cp = pltpu.make_async_copy(src.at[:, cols], dst.at[:, cols], in_sem.at[n, c])
            cp.start()
            row.append(cp)
        ins.append(row)

    barrier = pltpu.get_barrier_semaphore()
    for other in (up, down):
        pl.semaphore_signal(barrier, inc=1, device_id=(other, h), device_id_type=MESH)
    for step in range(1, 8):
        other = base + lax.rem(j + step, 8)
        pl.semaphore_signal(barrier, inc=1, device_id=(other, h), device_id_type=MESH)
    for zz in range(n_zx):
        for hh in range(2):
            other = zz * 8 + y * 2 + lax.rem(zx, 2)

            @pl.when(jnp.logical_or(other != d, h != hh))
            def _():
                pl.semaphore_signal(barrier, inc=1, device_id=(other, hh), device_id_type=MESH)

    flip = (iota((ROWS, ROWS), 0) + iota((ROWS, ROWS), 1) == ROWS - 1).astype(F32).astype(BF16)
    fr, fc = iota((ROWS, 2 * ROWS), 0), iota((ROWS, 2 * ROWS), 1) % ROWS
    flip2 = (jnp.logical_and(fr // BLK == fc // BLK, fr % BLK + fc % BLK == BLK - 1)).astype(F32).astype(BF16)
    for g in range(8):
        mask_ref[g] = (iota((BLK, 128), 1) // BLK == g).astype(F32).astype(BF16)

    def far(n, c):
        ref, target, slot = ((x_ref, up, 2), (dc_ref, down, 2))[n]
        cs = pl.ds(c * PER, PER)
        return pltpu.make_async_remote_copy(
            src_ref=ref.at[0, cs], dst_ref=ref.at[slot, cs],
            send_sem=far_send.at[n, c], recv_sem=far_recv.at[n, c],
            device_id=(target, h), device_id_type=MESH,
        )

    def near(n, c, src_slot):
        ref = (x_ref, dc_ref)[n]
        cs = pl.ds(c * PER, PER)
        return pltpu.make_async_remote_copy(
            src_ref=ref.at[src_slot, cs], dst_ref=ref.at[1, cs],
            send_sem=near_send.at[n, c], recv_sem=near_recv.at[n, c],
            device_id=(mate, h), device_id_type=MESH,
        )

    for c in range(CHUNKS):
        for cp in ins[c]:
            cp.wait()

        def gate(n, carry):
            ls = lane_slice(n)
            st = (k_ref[:, ls].astype(F32) * v_ref[:, ls].astype(F32)).astype(BF16)
            dc_ref[0, n] = (g_ref[:, ls].astype(F32) * q_ref[:, ls].astype(F32)).astype(BF16)
            x_ref[0, n] = jnp.dot(flip, st, preferred_element_type=F32).astype(BF16)
            return carry

        lax.fori_loop(c * PER, (c + 1) * PER, gate, 0)
        if c == 0:
            pl.semaphore_wait(barrier, 9 + 2 * n_zx - to_self.astype(jnp.int32))
        far(0, c).start()
        far(1, c).start()

        @pl.when(core == 0)
        def _():
            near(0, c, 0).start()

        @pl.when(core == 1)
        def _():
            near(1, c, 0).start()

    s_ref[...] = jnp.zeros_like(s_ref)
    sh_ref[...] = jnp.zeros_like(sh_ref)
    taps = filt_ref[...].astype(BF16)
    ln = iota((288, 128), 1) % BLK

    def table(n, carry):
        e = (iota((128, 128), 0) == 8 * n + iota((128, 128), 1) // BLK).astype(F32).astype(BF16)
        f = jnp.dot(taps, e, preferred_element_type=F32)
        z = jnp.concatenate([jnp.zeros((16, 128), F32), f, jnp.zeros((16, 128), F32)], axis=0)
        amt = 15 - ln
        for b in (8, 4, 2, 1):
            sh_ref[8:296] = z
            z = jnp.where((amt & b) != 0, sh_ref[8 - b : 296 - b], z)
        zb = z.astype(BF16)
        for u in range(SPAN):
            s_ref[n, :, (NB - 1 + u) * 128 : (NB + u) * 128] = zb[16 + 16 * u : 32 + 16 * u]
        return carry

    lax.fori_loop(0, TILES, table, 0)

    def spread(block):
        n_u = block.shape[0] // BLK
        wide = block.reshape(n_u, 1, BLK, 128) * mask_ref[...][None]
        return wide.reshape(n_u * 128, 128)

    def operator(n, u0, n_u):
        return jnp.concatenate(
            [s_ref[n, :, (NB - 1 - i + u0) * 128 : (NB - 1 - i + u0 + n_u) * 128] for i in range(NB)], axis=0
        )

    def own(n, carry):
        rhs = jnp.concatenate([spread(x_ref[0, n]), spread(dc_ref[0, n])], axis=1)
        o_ref[n] = jnp.dot(operator(n, 0, NB), rhs, preferred_element_type=F32)
        return carry

    lax.fori_loop(0, TILES, own, 0)
    d_ref[...] = jnp.zeros_like(d_ref)

    ln2 = 15 - iota((264, 128), 1) % BLK

    def filter_terms(n, carry):
        dc = jnp.concatenate([dc_ref[0, n], dc_ref[1, n], dc_ref[2, n]], axis=0)
        lhs = jnp.concatenate([dc[BLK * i : BLK * i + SPAN * BLK] for i in range(NB)], axis=1)
        st = spread(x_ref[0, n])
        rhs = jnp.concatenate([st[(NB - 1 - i) * 128 : (NB - i) * 128] for i in range(NB)], axis=1)
        z = lax.dot_general(lhs, rhs, (((1,), (1,)), ((), ())), preferred_element_type=F32)
        sh_ref[0:272] = z
        z = jnp.where((ln2 & 8) != 0, sh_ref[8:272], z[:264])
        for b in (4, 2, 1):
            sh_ref[0:264] = z
            z = jnp.where((ln2 & b) != 0, sh_ref[b : 264 + b], z)
        z = z[:TAPS]
        hi = z.astype(BF16)
        lo = (z - hi.astype(F32)).astype(BF16)
        gr = iota((256, 128), 0) % 128
        g = (iota((256, 128), 1) == 8 * n + gr // BLK).astype(F32).astype(BF16)
        d_ref[...] += jnp.dot(jnp.concatenate([hi, lo], axis=1), g, preferred_element_type=F32)
        return carry

    def rest(n, carry):
        rx = jnp.concatenate([spread(x_ref[1, n]), spread(x_ref[2, n])], axis=0)
        rd = jnp.concatenate([spread(dc_ref[1, n]), spread(dc_ref[2, n])], axis=0)
        out = o_ref[n] + jnp.dot(
            operator(n, NB, 2 * NB), jnp.concatenate([rx, rd], axis=1), preferred_element_type=F32
        )
        ls = lane_slice(n)
        conv = jnp.concatenate([out[BLK * (NB - 1 - i) : BLK * (NB - i), :128] for i in range(NB)], axis=0)
        ds = out[:, 128:]
        hi = ds.astype(BF16)
        lo = (ds - hi.astype(F32)).astype(BF16)
        ds = jnp.dot(flip2, jnp.concatenate([hi, lo], axis=0), preferred_element_type=F32)
        kf, vf = k_ref[:, ls].astype(F32), v_ref[:, ls].astype(F32)
        qf, gf = q_ref[:, ls].astype(F32), g_ref[:, ls].astype(F32)
        skip = skip_ref[:, ls]
        conv = conv + skip * (kf * vf).astype(BF16).astype(F32)
        ds = ds + skip * dc_ref[0, n].astype(F32)
        mo_ref[:, ls] = (qf * conv).astype(BF16)
        qg_ref[:, ls] = (gf * conv).astype(BF16)
        kg_ref[:, ls] = (ds * vf).astype(BF16)
        vg_ref[:, ls] = (ds * kf).astype(BF16)
        return carry

    outs = []

    def finish(c):
        lax.fori_loop(c * PER, (c + 1) * PER, rest, 0)
        cols = pl.ds(c * PER * 128, PER * 128)
        for n, (src, dst) in enumerate(((mo_ref, mo_hbm), (qg_ref, qg_hbm), (kg_ref, kg_hbm), (vg_ref, vg_hbm))):
            cp = pltpu.make_async_copy(src.at[:, cols], dst.at[:, cols], out_sem.at[n, c])
            cp.start()
            outs.append(cp)

    def stage1(step):
        other = lax.rem(j + step, 8)
        return pltpu.make_async_remote_copy(
            src_ref=d1_ref.at[other], dst_ref=r1_ref.at[j],
            send_sem=s1_send.at[step], recv_sem=s1_recv.at[j],
            device_id=(base + other, h), device_id_type=MESH,
        )

    def stage1_arrival(step):
        other = lax.rem(j + step, 8)
        return pltpu.make_async_remote_copy(
            src_ref=d1_ref.at[other], dst_ref=r1_ref.at[other],
            send_sem=s1_send.at[step], recv_sem=s1_recv.at[other],
            device_id=(base + other, h), device_id_type=MESH,
        )

    for c in range(CHUNKS + 1):
        if c < CHUNKS:
            cs = pl.ds(c * PER, PER)
            far(0, c).wait_recv()
            far(1, c).wait_recv()

            @pl.when(d < 2)
            def _():
                x_ref[2, cs] = jnp.zeros((PER, 128, 128), BF16)

            @pl.when(d >= n_ctx - 2)
            def _():
                dc_ref[2, cs] = jnp.zeros((PER, 128, 128), BF16)

            @pl.when(core == 1)
            def _():
                near(0, c, 2).start()

            @pl.when(core == 0)
            def _():
                near(1, c, 2).start()

        if c > 0:
            near(0, c - 1, 0).wait_recv()
            near(1, c - 1, 0).wait_recv()
            lax.fori_loop((c - 1) * PER, c * PER, filter_terms, 0)
            if c == CHUNKS:
                for yy in range(4):
                    for cc in range(2):
                        for qq in range(n_q):
                            m = (2 * qq + cc) * 4 + yy
                            d1_ref[yy * 2 + cc, qq] = d_ref[8 * m : 8 * m + 8]
                for step in range(1, 8):
                    stage1(step).start()
            finish(c - 1)

    total = d1_ref[j]
    for step in range(1, 8):
        stage1_arrival(step).wait_recv()
        total = total + r1_ref[lax.rem(j + step, 8)]
    a1_ref[...] = total * scale

    def stage2(qq, cc, hh):
        n = (qq * 2 + cc) * 2 + hh
        target = (2 * qq + core) * 8 + y * 2 + cc
        return n, target, pltpu.make_async_remote_copy(
            src_ref=a1_ref.at[qq], dst_ref=r2_ref.at[zx * 2 + h],
            send_sem=s2_send.at[n], recv_sem=s2_recv.at[zx * 2 + h],
            device_id=(target, hh), device_id_type=MESH,
        )

    for qq in range(n_q):
        for cc in range(2):
            for hh in range(2):
                n, target, cp = stage2(qq, cc, hh)
                mine = jnp.logical_and(target == d, h == hh)

                @pl.when(jnp.logical_not(mine))
                def _():
                    cp.start()

                @pl.when(mine)
                def _():
                    r2_ref[zx * 2 + h] = a1_ref[qq]

    for zz in range(n_zx):
        for hh in range(2):
            other = zz * 8 + y * 2 + lax.rem(zx, 2)

            @pl.when(jnp.logical_or(other != d, h != hh))
            def _():
                pltpu.make_async_remote_copy(
                    src_ref=a1_ref.at[0], dst_ref=r2_ref.at[zz * 2 + hh],
                    send_sem=s2_send.at[0], recv_sem=s2_recv.at[zz * 2 + hh],
                    device_id=(other, hh), device_id_type=MESH,
                ).wait_recv()

    for hh in range(2):
        total = r2_ref[hh]
        for zz in range(1, n_zx):
            total = total + r2_ref[zz * 2 + hh]
        fg_ref[:, hh * 128 : (hh + 1) * 128] = jnp.where(core == 0, total[:4], total[4:])

    for cp in outs:
        cp.wait()
    for c in range(CHUNKS):
        for n in range(2):
            far(n, c).wait_send()
            near(n, c, 0).wait_send()
    for step in range(1, 8):
        stage1(step).wait_send()
    for qq in range(n_q):
        for cc in range(2):
            for hh in range(2):
                n, target, cp = stage2(qq, cc, hh)

                @pl.when(jnp.logical_or(target != d, h != hh))
                def _():
                    cp.wait_send()


def shards(q_proj, k_proj, v_proj, filt, skip, grad_out):
    n_ctx = lax.axis_size("ctx")
    scale = 1.0 / (16.0 * ROWS * n_ctx) ** 0.5
    any_spec = pl.BlockSpec(memory_space=pl.ANY)
    vmem = pl.BlockSpec(memory_space=pltpu.VMEM)
    big = jax.ShapeDtypeStruct((ROWS, LANES), BF16)
    n_q = n_ctx // 16
    outs = pl.pallas_call(
        functools.partial(kernel, n_ctx, scale),
        out_shape=(big, big, big, big, jax.ShapeDtypeStruct((4, 256), F32)),
        in_specs=[any_spec, any_spec, any_spec, vmem, vmem, any_spec],
        out_specs=(any_spec, any_spec, any_spec, any_spec, vmem),
        scratch_shapes=[pltpu.VMEM((ROWS, LANES), BF16)] * 4
        + [
            pltpu.VMEM((3, TILES, ROWS, 128), BF16),
            pltpu.VMEM((3, TILES, ROWS, 128), BF16),
            pltpu.VMEM((TILES, BLK, SLOTS * 128), BF16),
            pltpu.VMEM((TILES, ROWS, 256), F32),
            pltpu.VMEM((8, BLK, 128), BF16),
            pltpu.VMEM((304, 128), F32),
            pltpu.VMEM((TAPS, 128), F32),
            pltpu.VMEM((8, n_q, 8, 128), F32),
            pltpu.VMEM((8, n_q, 8, 128), F32),
            pltpu.VMEM((n_q, 8, 128), F32),
            pltpu.VMEM((n_q * 4, 8, 128), F32),
        ]
        + [pltpu.VMEM((ROWS, LANES), BF16)] * 4
        + [
            pltpu.SemaphoreType.DMA((4, CHUNKS)),
            pltpu.SemaphoreType.DMA((4, CHUNKS)),
            pltpu.SemaphoreType.DMA((2, CHUNKS)),
            pltpu.SemaphoreType.DMA((2, CHUNKS)),
            pltpu.SemaphoreType.DMA((2, CHUNKS)),
            pltpu.SemaphoreType.DMA((2, CHUNKS)),
            pltpu.SemaphoreType.DMA((8,)),
            pltpu.SemaphoreType.DMA((8,)),
            pltpu.SemaphoreType.DMA((16,)),
            pltpu.SemaphoreType.DMA((16,)),
            pltpu.SemaphoreType.DMA,
        ],
        compiler_params=pltpu.CompilerParams(
            collective_id=0, has_side_effects=True, vmem_limit_bytes=48 * 1024 * 1024
        ),
        cost_estimate=pl.CostEstimate(flops=3 * 10**9, bytes_accessed=4 * 2**20, transcendentals=0),
        name="hyena",
    )(q_proj, k_proj, v_proj, filt, skip.reshape(1, LANES), grad_out)
    return tuple(outs)


def solution(mesh):
    in_specs = (
        P("ctx", "ch"),
        P("ctx", "ch"),
        P("ctx", "ch"),
        P(None, "ch"),
        P("ch"),
        P("ctx", "ch"),
    )
    out_specs = (P("ctx", "ch"), P("ctx", "ch"), P("ctx", "ch"), P("ctx", "ch"), P("ctx", None))
    return jax.shard_map(shards, mesh=mesh, in_specs=in_specs, out_specs=out_specs, check_vma=False)
```

```python
import functools

import jax
import jax.numpy as jnp
from jax import lax
from jax.experimental import pallas as pl
from jax.experimental.pallas import tpu as pltpu
from jax.sharding import PartitionSpec as P

MESH = pl.DeviceIdType.MESH
F32 = jnp.float32
BF16 = jnp.bfloat16
ROWS = 128
LANES = 2048
TILES = LANES // 128
CHUNKS = 8
HALF = CHUNKS // 2
PER = TILES // CHUNKS
WIDTH = PER * 128
BLK = 16
NB = ROWS // BLK
TAPS = 256
SPAN = TAPS // BLK + 1
SLOTS = SPAN + 2 * (NB - 1)


def iota(shape, dim):
    return lax.broadcasted_iota(jnp.int32, shape, dim)


def kernel(
    n_ctx, scale,
    q_hbm, k_hbm, v_hbm, filt_hbm, skip_hbm, g_hbm,
    mo_ref, qg_ref, kg_ref, vg_ref, fg_ref,
    q_ref, k_ref, v_ref, g_ref, filt_ref, skip_ref,
    x_ref, dc_ref, s_ref, o_ref, mask_ref, sh_ref,
    d_ref, r1_ref, a1_ref, r2_ref,
    in_sem, small_sem, far_send, far_recv, near_send, near_recv,
    s1_send, s1_recv, s2_send, s2_recv,
):
    d = lax.axis_index("ctx")
    h = lax.axis_index("ch")
    up = lax.rem(d + 2, n_ctx)
    down = lax.rem(d + n_ctx - 2, n_ctx)
    core = lax.rem(d, 2)
    mate = d + 1 - 2 * core
    n_zx = n_ctx // 8
    zx = lax.div(d, 8)
    j = lax.rem(d, 8)
    e = j * 2 + h

    def turn(n, p):
        return (p + HALF) % CHUNKS if n == 0 else p

    def load(n, p):
        src, dst = ((k_hbm, k_ref), (v_hbm, v_ref), (g_hbm, g_ref), (q_hbm, q_ref))[n]
        cols = pl.ds(turn(n // 2, p) * WIDTH, WIDTH)
        return pltpu.make_async_copy(src.at[:, cols], dst.at[:, cols], in_sem.at[n, p])

    for p in range(CHUNKS):
        for n in range(4):
            load(n, p).start()
    load_filt = pltpu.make_async_copy(filt_hbm, filt_ref, small_sem.at[0])
    load_skip = pltpu.make_async_copy(skip_hbm, skip_ref, small_sem.at[1])
    load_filt.start()
    load_skip.start()

    def stage1_peer(step):
        return lax.rem(zx + step, n_zx)

    def stage2_peer(step):
        other = lax.rem(e + step, 16)
        return other, zx * 8 + lax.div(other, 2), lax.rem(other, 2)

    barrier = pltpu.get_barrier_semaphore()
    peers = [(up, h), (down, h)]
    peers += [(stage1_peer(step) * 8 + j, h) for step in range(1, n_zx)]
    peers += [stage2_peer(step)[1:] for step in range(1, 16)]
    for peer in peers:
        pl.semaphore_signal(barrier, inc=1, device_id=peer, device_id_type=MESH)

    flip = (iota((ROWS, ROWS), 0) + iota((ROWS, ROWS), 1) == ROWS - 1).astype(F32).astype(BF16)
    fr, fc = iota((ROWS, 2 * ROWS), 0), iota((ROWS, 2 * ROWS), 1) % ROWS
    flip2 = (jnp.logical_and(fr // BLK == fc // BLK, fr % BLK + fc % BLK == BLK - 1)).astype(F32).astype(BF16)
    for g in range(8):
        mask_ref[g] = (iota((BLK, 128), 1) // BLK == g).astype(F32).astype(BF16)

    def far(n, c):
        ref, target = ((x_ref, up), (dc_ref, down))[n]
        cs = pl.ds(c * PER, PER)
        return pltpu.make_async_remote_copy(
            src_ref=ref.at[0, cs], dst_ref=ref.at[2, cs],
            send_sem=far_send.at[n, c], recv_sem=far_recv.at[n, c],
            device_id=(target, h), device_id_type=MESH,
        )

    def near(n, c, src_slot):
        ref = (x_ref, dc_ref)[n]
        cs = pl.ds(c * PER, PER)
        return pltpu.make_async_remote_copy(
            src_ref=ref.at[src_slot, cs], dst_ref=ref.at[1, cs],
            send_sem=near_send.at[n, c], recv_sem=near_recv.at[n, c],
            device_id=(mate, h), device_id_type=MESH,
        )

    for p in range(CHUNKS):
        c0, c1 = turn(0, p), turn(1, p)
        load(0, p).wait()
        load(1, p).wait()
        cols = pl.ds(c0 * WIDTH, WIDTH)
        st = (k_ref[:, cols].astype(F32) * v_ref[:, cols].astype(F32)).astype(BF16)
        st = jnp.dot(flip, st, preferred_element_type=F32).astype(BF16)
        for t in range(PER):
            x_ref[0, c0 * PER + t] = st[:, t * 128 : (t + 1) * 128]
        load(2, p).wait()
        load(3, p).wait()
        cols = pl.ds(c1 * WIDTH, WIDTH)
        dc = (g_ref[:, cols].astype(F32) * q_ref[:, cols].astype(F32)).astype(BF16)
        for t in range(PER):
            dc_ref[0, c1 * PER + t] = dc[:, t * 128 : (t + 1) * 128]
        if p == 0:
            pl.semaphore_wait(barrier, len(peers))
        far(0, c0).start()
        far(1, c1).start()

        @pl.when(core == 0)
        def _():
            near(0, c0, 0).start()

        @pl.when(core == 1)
        def _():
            near(1, c1, 0).start()

    load_filt.wait()
    load_skip.wait()
    s_ref[:, :, : (NB - 1) * 128] = jnp.zeros((TILES, BLK, (NB - 1) * 128), BF16)
    s_ref[:, :, (NB - 1 + SPAN) * 128 :] = jnp.zeros((TILES, BLK, (NB - 1) * 128), BF16)
    sh_ref[...] = jnp.zeros_like(sh_ref)
    taps = filt_ref[...].astype(BF16)
    amt = 15 - iota((288, 128), 1) % BLK

    def table(c, carry):
        spots = iota((128, 512), 0) == 32 * c + iota((128, 512), 1) // BLK
        f = jnp.dot(taps, spots.astype(F32).astype(BF16), preferred_element_type=F32)
        edge = jnp.zeros((16, 128), F32)
        for t in range(4):
            z = jnp.concatenate([edge, f[:, t * 128 : (t + 1) * 128], edge], axis=0)
            for b in (8, 4, 2, 1):
                sh_ref[t, 8:296] = z
                z = jnp.where((amt & b) != 0, sh_ref[t, 8 - b : 296 - b], z)
            zb = z.astype(BF16)
            for u in range(SPAN):
                s_ref[c * 4 + t, :, (NB - 1 + u) * 128 : (NB + u) * 128] = zb[16 + 16 * u : 32 + 16 * u]
        return carry

    lax.fori_loop(0, TILES // 4, table, 0)

    def spread(block):
        n_u = block.shape[0] // BLK
        wide = block.reshape(n_u, 1, BLK, 128) * mask_ref[...][None]
        return wide.reshape(n_u * 128, 128)

    def operator(n, u0, n_u):
        return jnp.concatenate(
            [s_ref[n, :, (NB - 1 - i + u0) * 128 : (NB - 1 - i + u0 + n_u) * 128] for i in range(NB)], axis=0
        )

    def own(c, carry):
        for t in range(4):
            n = c * 4 + t
            rhs = jnp.concatenate([spread(x_ref[0, n]), spread(dc_ref[0, n])], axis=1)
            o_ref[n] = jnp.dot(operator(n, 0, NB), rhs, preferred_element_type=F32)
        return carry

    amt2 = 15 - iota((264, 128), 1) % BLK

    def filter_terms(p):
        tiles = [(p * PER + t, dc_ref, x_ref) for t in range(PER)]
        tiles += [((p + HALF) * PER + t, x_ref, dc_ref) for t in range(PER)]
        parts, spots = [], []
        for t, (n, long, short) in enumerate(tiles):
            rows = jnp.concatenate([long[0, n], long[1, n], long[2, n]], axis=0)
            lhs = jnp.concatenate([rows[BLK * i : BLK * i + SPAN * BLK] for i in range(NB)], axis=1)
            st = spread(short[0, n])
            rhs = jnp.concatenate([st[(NB - 1 - i) * 128 : (NB - i) * 128] for i in range(NB)], axis=1)
            sh_ref[t, 0:272] = lax.dot_general(lhs, rhs, (((1,), (1,)), ((), ())), preferred_element_type=F32)
        for t, (n, long, short) in enumerate(tiles):
            z = jnp.where((amt2 & 8) != 0, sh_ref[t, 8:272], sh_ref[t, 0:264])
            for b in (4, 2, 1):
                sh_ref[t, 0:264] = z
                z = jnp.where((amt2 & b) != 0, sh_ref[t, b : 264 + b], z)
            z = z[:TAPS]
            hi = z.astype(BF16)
            parts += [hi, (z - hi.astype(F32)).astype(BF16)]
            spot = (iota((256, 128), 1) == 8 * n + iota((256, 128), 0) % 128 // BLK).astype(F32)
            spots.append(spot.astype(BF16))
        terms = jnp.dot(
            jnp.concatenate(parts, axis=1), jnp.concatenate(spots, axis=0), preferred_element_type=F32
        )
        if p == 0:
            d_ref[...] = terms
        else:
            d_ref[...] += terms

    def rest(p):
        tiles = [p * PER + t for t in range(PER)] + [(p + HALF) * PER + t for t in range(PER)]
        his, los = [], []
        for n in tiles:
            rx = jnp.concatenate([spread(x_ref[1, n]), spread(x_ref[2, n])], axis=0)
            rd = jnp.concatenate([spread(dc_ref[1, n]), spread(dc_ref[2, n])], axis=0)
            out = o_ref[n] + jnp.dot(
                operator(n, NB, 2 * NB), jnp.concatenate([rx, rd], axis=1), preferred_element_type=F32
            )
            o_ref[n] = out
            ds = out[:, 128:]
            hi = ds.astype(BF16)
            his.append(hi)
            los.append((ds - hi.astype(F32)).astype(BF16))
        pair = jnp.concatenate([jnp.concatenate(his, axis=1), jnp.concatenate(los, axis=1)], axis=0)
        flipped = jnp.dot(flip2, pair, preferred_element_type=F32)
        for t, n in enumerate(tiles):
            ls = pl.ds(n * 128, 128)
            conv = jnp.concatenate(
                [o_ref[n, BLK * (NB - 1 - i) : BLK * (NB - i), :128] for i in range(NB)], axis=0
            )
            ds = flipped[:, t * 128 : (t + 1) * 128]
            kf, vf = k_ref[:, ls].astype(F32), v_ref[:, ls].astype(F32)
            qf, gf = q_ref[:, ls].astype(F32), g_ref[:, ls].astype(F32)
            skip = skip_ref[:, ls]
            conv = conv + skip * (kf * vf).astype(BF16).astype(F32)
            ds = ds + skip * dc_ref[0, n].astype(F32)
            mo_ref[:, ls] = (qf * conv).astype(BF16)
            qg_ref[:, ls] = (gf * conv).astype(BF16)
            kg_ref[:, ls] = (ds * vf).astype(BF16)
            vg_ref[:, ls] = (ds * kf).astype(BF16)

    def arrive(p):
        c0, c1 = turn(0, p), turn(1, p)
        far(0, c0).wait_recv()

        @pl.when(d < 2)
        def _():
            x_ref[2, pl.ds(c0 * PER, PER)] = jnp.zeros((PER, ROWS, 128), BF16)

        @pl.when(core == 1)
        def _():
            near(0, c0, 2).start()

        far(1, c1).wait_recv()

        @pl.when(d >= n_ctx - 2)
        def _():
            dc_ref[2, pl.ds(c1 * PER, PER)] = jnp.zeros((PER, ROWS, 128), BF16)

        @pl.when(core == 0)
        def _():
            near(1, c1, 2).start()

    def complete(p):
        near(0, turn(0, p), 0).wait_recv()
        near(1, turn(1, p), 0).wait_recv()

    def stage1(step):
        other = stage1_peer(step)
        return pltpu.make_async_remote_copy(
            src_ref=d_ref.at[pl.ds(other * 32, 32)], dst_ref=r1_ref.at[zx],
            send_sem=s1_send.at[step], recv_sem=s1_recv.at[zx],
            device_id=(other * 8 + j, h), device_id_type=MESH,
        )

    def stage1_from(step):
        other = stage1_peer(step)
        return pltpu.make_async_remote_copy(
            src_ref=d_ref.at[pl.ds(other * 32, 32)], dst_ref=r1_ref.at[other],
            send_sem=s1_send.at[step], recv_sem=s1_recv.at[other],
            device_id=(other * 8 + j, h), device_id_type=MESH,
        )

    def stage2(step):
        other, ctx, ch = stage2_peer(step)
        return pltpu.make_async_remote_copy(
            src_ref=a1_ref.at[lax.div(other, 4)], dst_ref=r2_ref.at[e],
            send_sem=s2_send.at[step], recv_sem=s2_recv.at[e],
            device_id=(ctx, ch), device_id_type=MESH,
        )

    def stage2_from(step):
        other, ctx, ch = stage2_peer(step)
        return pltpu.make_async_remote_copy(
            src_ref=a1_ref.at[lax.div(other, 4)], dst_ref=r2_ref.at[other],
            send_sem=s2_send.at[step], recv_sem=s2_recv.at[other],
            device_id=(ctx, ch), device_id_type=MESH,
        )

    lax.fori_loop(0, 2, own, 0)
    arrive(0)
    lax.fori_loop(2, 4, own, 0)
    for p in range(HALF):
        arrive(p + 1)
        complete(p)
        filter_terms(p)
    for step in range(1, n_zx):
        stage1(step).start()
    arrive(HALF + 1)
    complete(HALF)
    rest(0)

    total = d_ref[pl.ds(zx * 32, 32)]
    for step in range(1, n_zx):
        stage1_from(step).wait_recv()
        total = total + r1_ref[stage1_peer(step)]
    total = (total * scale).reshape(4, 8, 128)
    a1_ref[...] = total
    r2_ref[e] = a1_ref[lax.div(j, 2)]
    for step in range(1, 16):
        stage2(step).start()

    for p in range(1, HALF):
        if HALF + p + 1 < CHUNKS:
            arrive(HALF + p + 1)
        complete(HALF + p)
        rest(p)

    for step in range(1, 16):
        stage2_from(step).wait_recv()
    for hh in range(2):
        total = r2_ref[hh]
        for jj in range(1, 8):
            total = total + r2_ref[jj * 2 + hh]
        fg_ref[:, hh * 128 : (hh + 1) * 128] = jnp.where(core == 0, total[:4], total[4:])

    for c in range(CHUNKS):
        for n in range(2):
            far(n, c).wait_send()
            near(n, c, 0).wait_send()
    for step in range(1, n_zx):
        stage1(step).wait_send()
    for step in range(1, 16):
        stage2(step).wait_send()


def hand_over(*refs):
    src, dst, buf = refs[:5], refs[5:10], refs[10:15]
    in_sem, out_sem = refs[15:]
    steps = [(i, pl.ds(c * 512, 512)) for c in range(4) for i in range(4)] + [(4, pl.ds(0, 256))]
    first = [pltpu.make_async_copy(src[i].at[:, c], buf[i].at[:, c], in_sem.at[n]) for n, (i, c) in enumerate(steps)]
    then = [pltpu.make_async_copy(buf[i].at[:, c], dst[i].at[:, c], out_sem.at[n]) for n, (i, c) in enumerate(steps)]
    for copy in first:
        copy.start()
    for copy, onward in zip(first, then):
        copy.wait()
        onward.start()
    for onward in then:
        onward.wait()


def shards(q_proj, k_proj, v_proj, filt, skip, grad_out):
    n_ctx = lax.axis_size("ctx")
    scale = 1.0 / (16.0 * ROWS * n_ctx) ** 0.5
    hbm = pl.BlockSpec(memory_space=pltpu.HBM)
    anywhere = pl.BlockSpec(memory_space=pl.ANY)
    vmem = pl.BlockSpec(memory_space=pltpu.VMEM)
    big = jax.ShapeDtypeStruct((ROWS, LANES), BF16)
    results = (big, big, big, big, jax.ShapeDtypeStruct((4, 256), F32))
    n_zx = n_ctx // 8
    outs = pl.pallas_call(
        functools.partial(kernel, n_ctx, scale),
        out_shape=results,
        in_specs=[hbm] * 6,
        out_specs=(vmem,) * 5,
        scratch_shapes=[pltpu.VMEM((ROWS, LANES), BF16)] * 4
        + [
            pltpu.VMEM((TAPS, 128), F32),
            pltpu.VMEM((1, LANES), F32),
            pltpu.VMEM((3, TILES, ROWS, 128), BF16),
            pltpu.VMEM((3, TILES, ROWS, 128), BF16),
            pltpu.VMEM((TILES, BLK, SLOTS * 128), BF16),
            pltpu.VMEM((TILES, ROWS, 256), F32),
            pltpu.VMEM((8, BLK, 128), BF16),
            pltpu.VMEM((4, 304, 128), F32),
            pltpu.VMEM((TAPS, 128), F32),
            pltpu.VMEM((n_zx, 32, 128), F32),
            pltpu.VMEM((4, 8, 128), F32),
            pltpu.VMEM((16, 8, 128), F32),
            pltpu.SemaphoreType.DMA((4, CHUNKS)),
            pltpu.SemaphoreType.DMA((2,)),
            pltpu.SemaphoreType.DMA((2, CHUNKS)),
            pltpu.SemaphoreType.DMA((2, CHUNKS)),
            pltpu.SemaphoreType.DMA((2, CHUNKS)),
            pltpu.SemaphoreType.DMA((2, CHUNKS)),
            pltpu.SemaphoreType.DMA((n_zx,)),
            pltpu.SemaphoreType.DMA((n_zx,)),
            pltpu.SemaphoreType.DMA((16,)),
            pltpu.SemaphoreType.DMA((16,)),
        ],
        compiler_params=pltpu.CompilerParams(
            collective_id=0, has_side_effects=True, vmem_limit_bytes=60 * 1024 * 1024
        ),
        cost_estimate=pl.CostEstimate(flops=3 * 10**9, bytes_accessed=4 * 2**20, transcendentals=0),
        name="hyena",
    )(q_proj, k_proj, v_proj, filt, skip.reshape(1, LANES), grad_out)
    outs = pl.pallas_call(
        hand_over,
        out_shape=results,
        in_specs=[hbm] * 5,
        out_specs=(hbm,) * 5,
        scratch_shapes=[pltpu.VMEM(r.shape, r.dtype) for r in results] + [pltpu.SemaphoreType.DMA((17,))] * 2,
        compiler_params=pltpu.CompilerParams(vmem_limit_bytes=60 * 1024 * 1024),
        cost_estimate=pl.CostEstimate(flops=0, bytes_accessed=4 * 2**20, transcendentals=0),
        name="hand_over",
    )(*outs)
    return tuple(outs)


def solution(mesh):
    in_specs = (
        P("ctx", "ch"),
        P("ctx", "ch"),
        P("ctx", "ch"),
        P(None, "ch"),
        P("ch"),
        P("ctx", "ch"),
    )
    out_specs = (P("ctx", "ch"), P("ctx", "ch"), P("ctx", "ch"), P("ctx", "ch"), P("ctx", None))
    return jax.shard_map(shards, mesh=mesh, in_specs=in_specs, out_specs=out_specs, check_vma=False)
```

```python
import functools

import jax
import jax.numpy as jnp
from jax import lax
from jax.experimental import pallas as pl
from jax.experimental.pallas import tpu as pltpu
from jax.sharding import PartitionSpec as P

MESH = pl.DeviceIdType.MESH
F32 = jnp.float32
BF16 = jnp.bfloat16
ROWS = 128
LANES = 2048
TILES = LANES // 128
CHUNKS = 8
HALF = CHUNKS // 2
SHEET = 16
PER = TILES // CHUNKS
WIDTH = PER * 128
BLK = 16
NB = ROWS // BLK
TAPS = 256
SPAN = TAPS // BLK + 1
SLOTS = SPAN + 2 * (NB - 1)


def iota(shape, dim):
    return lax.broadcasted_iota(jnp.int32, shape, dim)


def kernel(
    n_ctx, scale,
    q_hbm, k_hbm, v_hbm, filt_hbm, skip_hbm, g_hbm,
    mo_hbm, qg_hbm, kg_hbm, vg_hbm, fg_hbm,
    q_ref, k_ref, v_ref, g_ref, filt_ref, skip_ref,
    x_ref, dc_ref, s_ref, o_ref, mask_ref, sh_ref,
    d_ref, d1_ref, r1_ref, a1_ref, r2_ref,
    mo_ref, qg_ref, kg_ref, vg_ref, fg_ref,
    in_sem, out_sem, small_sem, far_send, far_recv, near_send, near_recv,
    s1_send, s1_recv, s2_send, s2_recv,
):
    d = lax.axis_index("ctx")
    h = lax.axis_index("ch")
    up = lax.rem(d + 2, n_ctx)
    down = lax.rem(d + n_ctx - 2, n_ctx)
    core = lax.rem(d, 2)
    mate = d + 1 - 2 * core
    layer = lax.div(d, 2 * SHEET)
    spot = lax.rem(lax.div(d, 2), SHEET)
    pile = 2 * n_ctx // SHEET
    e = (layer * 2 + core) * 2 + h

    def turn(n, p):
        return (p + HALF) % CHUNKS if n == 0 else p

    def load(n, part):
        src, dst = ((k_hbm, k_ref), (v_hbm, v_ref), (g_hbm, g_ref), (q_hbm, q_ref))[n]
        first, count = ((0, 1), (1, HALF - 1), (HALF, HALF))[part]
        cols = pl.ds(turn(n // 2, first) * WIDTH, count * WIDTH)
        return pltpu.make_async_copy(src.at[:, cols], dst.at[:, cols], in_sem.at[n, part])

    for n in range(4):
        load(n, 0).start()

    def stage1_peer(step):
        other = lax.rem(spot + step, SHEET)
        return other, (layer * SHEET + other) * 2 + core, h

    def stage2_peer(step):
        other = lax.rem(e + step, pile)
        ctx = (lax.div(other, 4) * SHEET + spot) * 2 + lax.rem(lax.div(other, 2), 2)
        return other, ctx, lax.rem(other, 2)

    barrier = pltpu.get_barrier_semaphore()
    peers = [(up, h), (down, h)]
    peers += [stage1_peer(step)[1:] for step in range(1, SHEET)]
    peers += [stage2_peer(step)[1:] for step in range(1, pile)]
    for peer in peers:
        pl.semaphore_signal(barrier, inc=1, device_id=peer, device_id_type=MESH)
    for part in range(1, 3):
        for n in range(4):
            load(n, part).start()
    load_filt = pltpu.make_async_copy(filt_hbm, filt_ref, small_sem.at[0])
    load_skip = pltpu.make_async_copy(skip_hbm, skip_ref, small_sem.at[1])
    load_filt.start()
    load_skip.start()

    flip = (iota((ROWS, ROWS), 0) + iota((ROWS, ROWS), 1) == ROWS - 1).astype(F32).astype(BF16)
    fr, fc = iota((ROWS, 2 * ROWS), 0), iota((ROWS, 2 * ROWS), 1) % ROWS
    flip2 = (jnp.logical_and(fr // BLK == fc // BLK, fr % BLK + fc % BLK == BLK - 1)).astype(F32).astype(BF16)
    for g in range(8):
        mask_ref[g] = (iota((BLK, 128), 1) // BLK == g).astype(F32).astype(BF16)

    def far(n, c):
        ref, target = ((x_ref, up), (dc_ref, down))[n]
        cs = pl.ds(c * PER, PER)
        return pltpu.make_async_remote_copy(
            src_ref=ref.at[0, cs], dst_ref=ref.at[2, cs],
            send_sem=far_send.at[n], recv_sem=far_recv.at[n, c],
            device_id=(target, h), device_id_type=MESH,
        )

    def near(n, c, src_slot):
        ref = (x_ref, dc_ref)[n]
        cs = pl.ds(c * PER, PER)
        return pltpu.make_async_remote_copy(
            src_ref=ref.at[src_slot, cs], dst_ref=ref.at[1, cs],
            send_sem=near_send.at[n], recv_sem=near_recv.at[n, c],
            device_id=(mate, h), device_id_type=MESH,
        )

    def gate(p):
        c0, c1 = turn(0, p), turn(1, p)
        part = {0: 0, 1: 1, HALF: 2}.get(p)
        if part is not None:
            load(0, part).wait()
            load(1, part).wait()
        cols = pl.ds(c0 * WIDTH, WIDTH)
        st = (k_ref[:, cols].astype(F32) * v_ref[:, cols].astype(F32)).astype(BF16)
        st = jnp.dot(flip, st, preferred_element_type=F32).astype(BF16)
        for t in range(PER):
            x_ref[0, c0 * PER + t] = st[:, t * 128 : (t + 1) * 128]
        if part is not None:
            load(2, part).wait()
            load(3, part).wait()
        cols = pl.ds(c1 * WIDTH, WIDTH)
        dc = (g_ref[:, cols].astype(F32) * q_ref[:, cols].astype(F32)).astype(BF16)
        for t in range(PER):
            dc_ref[0, c1 * PER + t] = dc[:, t * 128 : (t + 1) * 128]

    def send(p):
        c0, c1 = turn(0, p), turn(1, p)
        far(0, c0).start()
        far(1, c1).start()

        @pl.when(core == 0)
        def _():
            near(0, c0, 0).start()

        @pl.when(core == 1)
        def _():
            near(1, c1, 0).start()

    gate(0)
    pl.semaphore_wait(barrier, len(peers))
    send(0)
    for p in range(1, CHUNKS):
        gate(p)
        send(p)

    load_filt.wait()
    load_skip.wait()
    s_ref[:, :, : (NB - 1) * 128] = jnp.zeros((TILES, BLK, (NB - 1) * 128), BF16)
    s_ref[:, :, (NB - 1 + SPAN) * 128 :] = jnp.zeros((TILES, BLK, (NB - 1) * 128), BF16)
    sh_ref[...] = jnp.zeros_like(sh_ref)
    taps = filt_ref[...].astype(BF16)
    amt = 15 - iota((288, 128), 1) % BLK

    def table(c, carry):
        spots = iota((128, 512), 0) == 32 * c + iota((128, 512), 1) // BLK
        f = jnp.dot(taps, spots.astype(F32).astype(BF16), preferred_element_type=F32)
        edge = jnp.zeros((16, 128), F32)
        for t in range(4):
            z = jnp.concatenate([edge, f[:, t * 128 : (t + 1) * 128], edge], axis=0)
            for b in (8, 4, 2, 1):
                sh_ref[t, 8:296] = z
                z = jnp.where((amt & b) != 0, sh_ref[t, 8 - b : 296 - b], z)
            zb = z.astype(BF16)
            for u in range(SPAN):
                s_ref[c * 4 + t, :, (NB - 1 + u) * 128 : (NB + u) * 128] = zb[16 + 16 * u : 32 + 16 * u]
        return carry

    lax.fori_loop(0, TILES // 4, table, 0)

    def spread(block):
        n_u = block.shape[0] // BLK
        wide = block.reshape(n_u, 1, BLK, 128) * mask_ref[...][None]
        return wide.reshape(n_u * 128, 128)

    def operator(n, u0, n_u):
        return jnp.concatenate(
            [s_ref[n, :, (NB - 1 - i + u0) * 128 : (NB - 1 - i + u0 + n_u) * 128] for i in range(NB)], axis=0
        )

    def own(c, carry):
        for t in range(4):
            n = c * 4 + t
            rhs = jnp.concatenate([spread(x_ref[0, n]), spread(dc_ref[0, n])], axis=1)
            o_ref[n] = jnp.dot(operator(n, 0, NB), rhs, preferred_element_type=F32)
        return carry

    amt2 = 15 - iota((264, 128), 1) % BLK

    def filter_terms(p):
        tiles = [(p * PER + t, dc_ref, x_ref) for t in range(PER)]
        tiles += [((p + HALF) * PER + t, x_ref, dc_ref) for t in range(PER)]
        parts, spots = [], []
        for t, (n, long, short) in enumerate(tiles):
            rows = jnp.concatenate([long[0, n], long[1, n], long[2, n]], axis=0)
            lhs = jnp.concatenate([rows[BLK * i : BLK * i + SPAN * BLK] for i in range(NB)], axis=1)
            st = spread(short[0, n])
            rhs = jnp.concatenate([st[(NB - 1 - i) * 128 : (NB - i) * 128] for i in range(NB)], axis=1)
            sh_ref[t, 0:272] = lax.dot_general(lhs, rhs, (((1,), (1,)), ((), ())), preferred_element_type=F32)
        for t, (n, long, short) in enumerate(tiles):
            z = jnp.where((amt2 & 8) != 0, sh_ref[t, 8:272], sh_ref[t, 0:264])
            for b in (4, 2, 1):
                sh_ref[t, 0:264] = z
                z = jnp.where((amt2 & b) != 0, sh_ref[t, b : 264 + b], z)
            z = z[:TAPS]
            hi = z.astype(BF16)
            parts += [hi, (z - hi.astype(F32)).astype(BF16)]
            spot = (iota((256, 128), 1) == 8 * n + iota((256, 128), 0) % 128 // BLK).astype(F32)
            spots.append(spot.astype(BF16))
        terms = jnp.dot(
            jnp.concatenate(parts, axis=1), jnp.concatenate(spots, axis=0), preferred_element_type=F32
        )
        if p == 0:
            d_ref[...] = terms
        else:
            d_ref[...] += terms

    def store(n, c):
        src, dst = ((mo_ref, mo_hbm), (qg_ref, qg_hbm), (kg_ref, kg_hbm), (vg_ref, vg_hbm))[n]
        cols = pl.ds(c * WIDTH, WIDTH)
        return pltpu.make_async_copy(src.at[:, cols], dst.at[:, cols], out_sem.at[n])

    def rest(p):
        tiles = [p * PER + t for t in range(PER)] + [(p + HALF) * PER + t for t in range(PER)]
        his, los = [], []
        for n in tiles:
            rx = jnp.concatenate([spread(x_ref[1, n]), spread(x_ref[2, n])], axis=0)
            rd = jnp.concatenate([spread(dc_ref[1, n]), spread(dc_ref[2, n])], axis=0)
            out = o_ref[n] + jnp.dot(
                operator(n, NB, 2 * NB), jnp.concatenate([rx, rd], axis=1), preferred_element_type=F32
            )
            o_ref[n] = out
            ds = out[:, 128:]
            hi = ds.astype(BF16)
            his.append(hi)
            los.append((ds - hi.astype(F32)).astype(BF16))
        pair = jnp.concatenate([jnp.concatenate(his, axis=1), jnp.concatenate(los, axis=1)], axis=0)
        flipped = jnp.dot(flip2, pair, preferred_element_type=F32)
        for t, n in enumerate(tiles):
            ls = pl.ds(n * 128, 128)
            conv = jnp.concatenate(
                [o_ref[n, BLK * (NB - 1 - i) : BLK * (NB - i), :128] for i in range(NB)], axis=0
            )
            ds = flipped[:, t * 128 : (t + 1) * 128]
            kf, vf = k_ref[:, ls].astype(F32), v_ref[:, ls].astype(F32)
            qf, gf = q_ref[:, ls].astype(F32), g_ref[:, ls].astype(F32)
            skip = skip_ref[:, ls]
            conv = conv + skip * (kf * vf).astype(BF16).astype(F32)
            ds = ds + skip * dc_ref[0, n].astype(F32)
            mo_ref[:, ls] = (qf * conv).astype(BF16)
            qg_ref[:, ls] = (gf * conv).astype(BF16)
            kg_ref[:, ls] = (ds * vf).astype(BF16)
            vg_ref[:, ls] = (ds * kf).astype(BF16)
        for c in (p, p + HALF):
            for n in range(4):
                store(n, c).start()

    def arrive(p):
        c0, c1 = turn(0, p), turn(1, p)
        far(0, c0).wait_recv()

        @pl.when(d < 2)
        def _():
            x_ref[2, pl.ds(c0 * PER, PER)] = jnp.zeros((PER, ROWS, 128), BF16)

        @pl.when(core == 1)
        def _():
            near(0, c0, 2).start()

        far(1, c1).wait_recv()

        @pl.when(d >= n_ctx - 2)
        def _():
            dc_ref[2, pl.ds(c1 * PER, PER)] = jnp.zeros((PER, ROWS, 128), BF16)

        @pl.when(core == 0)
        def _():
            near(1, c1, 2).start()

    def complete(p):
        near(0, turn(0, p), 0).wait_recv()
        near(1, turn(1, p), 0).wait_recv()

    def stage1(step):
        other, ctx, ch = stage1_peer(step)
        return pltpu.make_async_remote_copy(
            src_ref=d1_ref.at[other], dst_ref=r1_ref.at[spot],
            send_sem=s1_send, recv_sem=s1_recv,
            device_id=(ctx, ch), device_id_type=MESH,
        )

    def stage2(step):
        other, ctx, ch = stage2_peer(step)
        return pltpu.make_async_remote_copy(
            src_ref=a1_ref.at[lax.div(other, 2)], dst_ref=r2_ref.at[e],
            send_sem=s2_send, recv_sem=s2_recv,
            device_id=(ctx, ch), device_id_type=MESH,
        )

    own(0, 0)
    for p in range(HALF):
        arrive(p)
        if p > 0:
            complete(p - 1)
            filter_terms(p - 1)
    complete(HALF - 1)
    filter_terms(HALF - 1)
    for n in range(SHEET):
        rows = [d_ref[pl.ds(z * 8 * SHEET + 8 * n, 8)] for z in range(pile // 4)]
        d1_ref[n] = jnp.concatenate(rows, axis=0).astype(BF16)
    for step in range(1, SHEET):
        stage1(step).start()
    arrive(4)
    own(1, 0)
    own(2, 0)
    own(3, 0)
    arrive(5)
    complete(4)
    rest(0)
    total = jnp.concatenate([d_ref[pl.ds(z * 8 * SHEET + 8 * spot, 8)] for z in range(pile // 4)], axis=0)
    others = r1_ref.at[pl.ds(0, SHEET - 1)]
    pltpu.make_async_copy(others, others, s1_recv).wait()
    for step in range(1, SHEET):
        total = total + r1_ref[stage1_peer(step)[0]].astype(F32)
    total = total * scale
    for n in range(pile // 2):
        a1_ref[n] = total[4 * n : 4 * n + 4]
    r2_ref[e] = a1_ref[lax.div(e, 2)]
    for step in range(1, pile):
        stage2(step).start()

    arrive(6)
    complete(5)
    rest(1)
    arrive(7)
    complete(6)
    rest(2)
    complete(7)
    rest(3)
    rest_of_pile = r2_ref.at[pl.ds(0, pile - 1)]
    pltpu.make_async_copy(rest_of_pile, rest_of_pile, s2_recv).wait()
    for hh in range(2):
        total = r2_ref[hh]
        for n in range(1, pile // 2):
            total = total + r2_ref[n * 2 + hh]
        fg_ref[:, hh * 128 : (hh + 1) * 128] = total

    last = pltpu.make_async_copy(fg_ref, fg_hbm, small_sem.at[0])
    last.start()

    for n, (src, dst) in enumerate(((mo_ref, mo_hbm), (qg_ref, qg_hbm), (kg_ref, kg_hbm), (vg_ref, vg_hbm))):
        pltpu.make_async_copy(src, dst, out_sem.at[n]).wait()
    for n in range(2):
        whole = (x_ref, dc_ref)[n].at[0]
        pltpu.make_async_copy(whole, whole, far_send.at[n]).wait()
        pltpu.make_async_copy(whole, whole, near_send.at[n]).wait()
    pltpu.make_async_copy(others, others, s1_send).wait()
    pltpu.make_async_copy(rest_of_pile, rest_of_pile, s2_send).wait()
    last.wait()


def hand_over(*refs):
    src, dst, buf, small = refs[:5], refs[5:10], refs[10], refs[11]
    in_sem, out_sem = refs[12:]
    place = [buf.at[i] for i in range(4)] + [small]
    first = [pltpu.make_async_copy(src[i], place[i], in_sem.at[i]) for i in range(5)]
    then = [pltpu.make_async_copy(place[i], dst[i], out_sem.at[i // 4]) for i in range(5)]
    for copy in first:
        copy.start()
    for copy, onward in zip(first, then):
        copy.wait()
        onward.start()
    pltpu.make_async_copy(buf, buf, out_sem.at[0]).wait()
    then[4].wait()


def shards(q_proj, k_proj, v_proj, filt, skip, grad_out):
    n_ctx = lax.axis_size("ctx")
    scale = 1.0 / (16.0 * ROWS * n_ctx) ** 0.5
    hbm = pl.BlockSpec(memory_space=pltpu.HBM)
    big = jax.ShapeDtypeStruct((ROWS, LANES), BF16)
    results = (big, big, big, big, jax.ShapeDtypeStruct((4, 256), F32))
    pile = 2 * n_ctx // SHEET
    outs = pl.pallas_call(
        functools.partial(kernel, n_ctx, scale),
        out_shape=results,
        in_specs=[hbm] * 6,
        out_specs=(hbm,) * 5,
        scratch_shapes=[pltpu.VMEM((ROWS, LANES), BF16)] * 4
        + [
            pltpu.VMEM((TAPS, 128), F32),
            pltpu.VMEM((1, LANES), F32),
            pltpu.VMEM((3, TILES, ROWS, 128), BF16),
            pltpu.VMEM((3, TILES, ROWS, 128), BF16),
            pltpu.VMEM((TILES, BLK, SLOTS * 128), BF16),
            pltpu.VMEM((TILES, ROWS, 256), F32),
            pltpu.VMEM((8, BLK, 128), BF16),
            pltpu.VMEM((4, 304, 128), F32),
            pltpu.VMEM((TAPS, 128), F32),
            pltpu.VMEM((SHEET, 2 * pile, 128), BF16),
            pltpu.VMEM((SHEET, 2 * pile, 128), BF16),
            pltpu.VMEM((pile // 2, 4, 128), F32),
            pltpu.VMEM((pile, 4, 128), F32),
        ]
        + [pltpu.VMEM((ROWS, LANES), BF16)] * 4
        + [
            pltpu.VMEM((4, 256), F32),
            pltpu.SemaphoreType.DMA((4, 3)),
            pltpu.SemaphoreType.DMA((4,)),
            pltpu.SemaphoreType.DMA((2,)),
            pltpu.SemaphoreType.DMA((2,)),
            pltpu.SemaphoreType.DMA((2, CHUNKS)),
            pltpu.SemaphoreType.DMA((2,)),
            pltpu.SemaphoreType.DMA((2, CHUNKS)),
            pltpu.SemaphoreType.DMA,
            pltpu.SemaphoreType.DMA,
            pltpu.SemaphoreType.DMA,
            pltpu.SemaphoreType.DMA,
        ],
        compiler_params=pltpu.CompilerParams(
            collective_id=0, has_side_effects=True, vmem_limit_bytes=60 * 1024 * 1024
        ),
        cost_estimate=pl.CostEstimate(flops=3 * 10**9, bytes_accessed=4 * 2**20, transcendentals=0),
        name="hyena",
    )(q_proj, k_proj, v_proj, filt, skip.reshape(1, LANES), grad_out)
    outs = pl.pallas_call(
        hand_over,
        out_shape=results,
        in_specs=[hbm] * 5,
        out_specs=(hbm,) * 5,
        scratch_shapes=[
            pltpu.VMEM((4, ROWS, LANES), BF16),
            pltpu.VMEM((4, 256), F32),
            pltpu.SemaphoreType.DMA((5,)),
            pltpu.SemaphoreType.DMA((2,)),
        ],
        compiler_params=pltpu.CompilerParams(vmem_limit_bytes=60 * 1024 * 1024),
        cost_estimate=pl.CostEstimate(flops=0, bytes_accessed=4 * 2**20, transcendentals=0),
        name="hand_over",
    )(*outs)
    return tuple(outs)


def solution(mesh):
    in_specs = (
        P("ctx", "ch"),
        P("ctx", "ch"),
        P("ctx", "ch"),
        P(None, "ch"),
        P("ch"),
        P("ctx", "ch"),
    )
    out_specs = (P("ctx", "ch"), P("ctx", "ch"), P("ctx", "ch"), P("ctx", "ch"), P("ctx", None))
    return jax.shard_map(shards, mesh=mesh, in_specs=in_specs, out_specs=out_specs, check_vma=False)
```

```python
import functools

import jax
import jax.numpy as jnp
from jax import lax
from jax.experimental import pallas as pl
from jax.experimental.pallas import tpu as pltpu
from jax.sharding import PartitionSpec as P

MESH = pl.DeviceIdType.MESH
F32 = jnp.float32
BF16 = jnp.bfloat16
ROWS = 128
LANES = 2048
TILES = LANES // 128
CHUNKS = 8
HALF = CHUNKS // 2
SHEET = 16
PER = TILES // CHUNKS
WIDTH = PER * 128
BLK = 16
NB = ROWS // BLK
TAPS = 256
SPAN = TAPS // BLK + 1
SLOTS = SPAN + 2 * (NB - 1)


def iota(shape, dim):
    return lax.broadcasted_iota(jnp.int32, shape, dim)


def kernel(
    n_ctx, scale,
    q_hbm, k_hbm, v_hbm, filt_hbm, skip_hbm, g_hbm,
    mo_hbm, qg_hbm, kg_hbm, vg_hbm, fg_hbm,
    q_ref, k_ref, v_ref, g_ref, filt_ref, skip_ref,
    x_ref, dc_ref, m_ref, s_ref, o_ref, mask_ref, sh_ref, z_ref, tsh_ref,
    d_ref, d1_ref, r1_ref, a1_ref, r2_ref,
    mo_ref, qg_ref, kg_ref, vg_ref, fg_ref,
    in_sem, out_sem, small_sem, far_send, far_recv, near_send, near_recv, mate_send, mate_recv,
    s1_send, s1_recv, s2_send, s2_recv,
):
    d = lax.axis_index("ctx")
    h = lax.axis_index("ch")
    up = lax.rem(d + 2, n_ctx)
    down = lax.rem(d + n_ctx - 2, n_ctx)
    core = lax.rem(d, 2)
    mate = d + 1 - 2 * core
    layer = lax.div(d, 2 * SHEET)
    spot = lax.rem(lax.div(d, 2), SHEET)
    pile = 2 * n_ctx // SHEET
    e = (layer * 2 + core) * 2 + h

    def turn(n, p):
        return (p + HALF) % CHUNKS if n == 0 else p

    def load(n, part):
        src, dst = ((k_hbm, k_ref), (v_hbm, v_ref), (g_hbm, g_ref), (q_hbm, q_ref))[n]
        first, count = ((0, 1), (1, HALF - 1), (HALF, HALF))[part]
        cols = pl.ds(turn(n // 2, first) * WIDTH, count * WIDTH)
        return pltpu.make_async_copy(src.at[:, cols], dst.at[:, cols], in_sem.at[n, part])

    for n in range(4):
        load(n, 0).start()

    def stage1_peer(step):
        other = lax.rem(spot + step, SHEET)
        return other, (layer * SHEET + other) * 2 + core, h

    def stage2_peer(step):
        other = lax.rem(e + step, pile)
        ctx = (lax.div(other, 4) * SHEET + spot) * 2 + lax.rem(lax.div(other, 2), 2)
        return other, ctx, lax.rem(other, 2)

    barrier = pltpu.get_barrier_semaphore()
    peers = [(up, h), (down, h)]
    peers += [stage1_peer(step)[1:] for step in range(1, SHEET)]
    peers += [stage2_peer(step)[1:] for step in range(1, pile)]
    for peer in peers:
        pl.semaphore_signal(barrier, inc=1, device_id=peer, device_id_type=MESH)
    for part in range(1, 3):
        for n in range(4):
            load(n, part).start()
    load_filt = pltpu.make_async_copy(filt_hbm, filt_ref, small_sem.at[0])
    load_skip = pltpu.make_async_copy(skip_hbm, skip_ref, small_sem.at[1])
    load_filt.start()
    load_skip.start()

    flip = (iota((ROWS, ROWS), 0) + iota((ROWS, ROWS), 1) == ROWS - 1).astype(F32).astype(BF16)
    fr, fc = iota((ROWS, 2 * ROWS), 0), iota((ROWS, 2 * ROWS), 1) % ROWS
    flip2 = (jnp.logical_and(fr // BLK == fc // BLK, fr % BLK + fc % BLK == BLK - 1)).astype(F32).astype(BF16)
    for g in range(8):
        mask_ref[g] = (iota((BLK, 128), 1) // BLK == g).astype(F32).astype(BF16)

    def far(n, c):
        ref, target = ((x_ref, up), (dc_ref, down))[n]
        cs = pl.ds(c * PER, PER)
        return pltpu.make_async_remote_copy(
            src_ref=ref.at[0, cs], dst_ref=ref.at[2, cs],
            send_sem=far_send.at[n], recv_sem=far_recv.at[n, c],
            device_id=(target, h), device_id_type=MESH,
        )

    def near(n, c, src_slot):
        ref = (x_ref, dc_ref)[n]
        cs = pl.ds(c * PER, PER)
        return pltpu.make_async_remote_copy(
            src_ref=ref.at[src_slot, cs], dst_ref=ref.at[1, cs],
            send_sem=near_send.at[n], recv_sem=near_recv.at[n, c],
            device_id=(mate, h), device_id_type=MESH,
        )

    def gate(p):
        c0, c1 = turn(0, p), turn(1, p)
        part = {0: 0, 1: 1, HALF: 2}.get(p)
        if part is not None:
            load(0, part).wait()
            load(1, part).wait()
        cols = pl.ds(c0 * WIDTH, WIDTH)
        st = (k_ref[:, cols].astype(F32) * v_ref[:, cols].astype(F32)).astype(BF16)
        st = jnp.dot(flip, st, preferred_element_type=F32).astype(BF16)
        for t in range(PER):
            x_ref[0, c0 * PER + t] = st[:, t * 128 : (t + 1) * 128]
        if part is not None:
            load(2, part).wait()
            load(3, part).wait()
        cols = pl.ds(c1 * WIDTH, WIDTH)
        dc = (g_ref[:, cols].astype(F32) * q_ref[:, cols].astype(F32)).astype(BF16)
        for t in range(PER):
            dc_ref[0, c1 * PER + t] = dc[:, t * 128 : (t + 1) * 128]

    def to_mate(n, p):
        ref = (x_ref, dc_ref)[n]
        return pltpu.make_async_remote_copy(
            src_ref=ref.at[0, pl.ds(turn(n, p) * PER, PER)], dst_ref=m_ref.at[n, pl.ds((p - HALF) * PER, PER)],
            send_sem=mate_send.at[n], recv_sem=mate_recv.at[n],
            device_id=(mate, h), device_id_type=MESH,
        )

    def send(p):
        c0, c1 = turn(0, p), turn(1, p)
        far(0, c0).start()
        far(1, c1).start()
        if p >= HALF:
            to_mate(0, p).start()
            to_mate(1, p).start()

        @pl.when(core == 0)
        def _():
            near(0, c0, 0).start()

        @pl.when(core == 1)
        def _():
            near(1, c1, 0).start()

    gate(0)
    pl.semaphore_wait(barrier, len(peers))
    send(0)
    for p in range(1, CHUNKS):
        gate(p)
        send(p)

    amt = 15 - iota((288, 128), 1) % BLK

    def table(c, carry):
        spots = iota((128, 512), 0) == 32 * c + iota((128, 512), 1) // BLK
        f = jnp.dot(filt_ref[...].astype(BF16), spots.astype(F32).astype(BF16), preferred_element_type=F32)
        edge = jnp.zeros((16, 128), F32)
        for t in range(4):
            z = jnp.concatenate([edge, f[:, t * 128 : (t + 1) * 128], edge], axis=0)
            for b in (8, 4, 2, 1):
                tsh_ref[t, 8:296] = z
                z = jnp.where((amt & b) != 0, tsh_ref[t, 8 - b : 296 - b], z)
            zb = z.astype(BF16)
            for u in range(SPAN):
                s_ref[c * 4 + t, :, (NB - 1 + u) * 128 : (NB + u) * 128] = zb[16 + 16 * u : 32 + 16 * u]
        return carry


    def spread(block):
        n_u = block.shape[0] // BLK
        wide = block.reshape(n_u, 1, BLK, 128) * mask_ref[...][None]
        return wide.reshape(n_u * 128, 128)

    def operator(n, u0, n_u):
        return jnp.concatenate(
            [s_ref[n, :, (NB - 1 - i + u0) * 128 : (NB - 1 - i + u0 + n_u) * 128] for i in range(NB)], axis=0
        )

    def own(c, carry):
        for t in range(4):
            n = c * 4 + t
            rhs = jnp.concatenate([spread(x_ref[0, n]), spread(dc_ref[0, n])], axis=1)
            o_ref[n] = jnp.dot(operator(n, 0, NB), rhs, preferred_element_type=F32)
        return carry

    amt2 = 15 - iota((264, 128), 1) % BLK
    even, odd = 1.0 - core.astype(F32), core.astype(F32)

    def filter_tiles(p):
        tiles = [(p * PER + t, dc_ref, x_ref, 0, even) for t in range(PER)]
        return tiles + [((p + HALF) * PER + t, x_ref, dc_ref, 1, odd) for t in range(PER)]

    def correlate(block, n, short, side):
        pad = jnp.zeros(((NB - 1) * BLK, 128), BF16)
        rows = jnp.concatenate([pad, block, pad], axis=0)
        lhs = jnp.concatenate([rows[BLK * i : BLK * i + (2 * NB - 1) * BLK] for i in range(NB)], axis=1)
        both = (spread(short[0, n]), spread(m_ref[side, n - side * HALF * PER]))
        rhs = [jnp.concatenate([b[(NB - 1 - i) * 128 : (NB - i) * 128] for i in range(NB)], axis=1) for b in both]
        rhs = jnp.concatenate(rhs, axis=0)
        return lax.dot_general(lhs, rhs, (((1,), (1,)), ((), ())), preferred_element_type=F32)

    def filter_near(p):
        for n, long, short, side, far_weight in filter_tiles(p):
            y = correlate(long[0, n], n, short, side)
            z_ref[n, 0:16] = y[112:128, :128]
            z_ref[n, 16:128] = y[128:240, :128] + (1.0 - far_weight) * y[0:112, 128:]
            z_ref[n, 128:256] = (1.0 - far_weight) * y[112:240, 128:]

    def filter_terms(p):
        tiles = filter_tiles(p)
        parts, spots = [], []
        for t, (n, long, short, side, far_weight) in enumerate(tiles):
            y = correlate(long[2, n], n, short, side)
            sh_ref[t, 0:16] = z_ref[n, 0:16]
            sh_ref[t, 16:144] = z_ref[n, 16:144] + far_weight * y[0:128, 128:]
            sh_ref[t, 144:256] = z_ref[n, 144:256] + far_weight * y[128:240, 128:] + y[0:112, :128]
            sh_ref[t, 256:272] = y[112:128, :128]
        for t, (n, long, short, side, far_weight) in enumerate(tiles):
            z = jnp.where((amt2 & 8) != 0, sh_ref[t, 8:272], sh_ref[t, 0:264])
            for b in (4, 2, 1):
                sh_ref[t, 0:264] = z
                z = jnp.where((amt2 & b) != 0, sh_ref[t, b : 264 + b], z)
            z = z[:TAPS]
            hi = z.astype(BF16)
            parts += [hi, (z - hi.astype(F32)).astype(BF16)]
            spot = (iota((256, 128), 1) == 8 * n + iota((256, 128), 0) % 128 // BLK).astype(F32)
            spots.append(spot.astype(BF16))
        terms = jnp.dot(
            jnp.concatenate(parts, axis=1), jnp.concatenate(spots, axis=0), preferred_element_type=F32
        )
        if p == 0:
            d_ref[...] = terms
        else:
            d_ref[...] += terms

    def store(n, c):
        src, dst = ((mo_ref, mo_hbm), (qg_ref, qg_hbm), (kg_ref, kg_hbm), (vg_ref, vg_hbm))[n]
        cols = pl.ds(c * WIDTH, WIDTH)
        return pltpu.make_async_copy(src.at[:, cols], dst.at[:, cols], out_sem.at[n])

    def rest(p):
        tiles = [p * PER + t for t in range(PER)] + [(p + HALF) * PER + t for t in range(PER)]
        his, los = [], []
        for n in tiles:
            rx = jnp.concatenate([spread(x_ref[1, n]), spread(x_ref[2, n])], axis=0)
            rd = jnp.concatenate([spread(dc_ref[1, n]), spread(dc_ref[2, n])], axis=0)
            out = o_ref[n] + jnp.dot(
                operator(n, NB, 2 * NB), jnp.concatenate([rx, rd], axis=1), preferred_element_type=F32
            )
            o_ref[n] = out
            ds = out[:, 128:]
            hi = ds.astype(BF16)
            his.append(hi)
            los.append((ds - hi.astype(F32)).astype(BF16))
        pair = jnp.concatenate([jnp.concatenate(his, axis=1), jnp.concatenate(los, axis=1)], axis=0)
        flipped = jnp.dot(flip2, pair, preferred_element_type=F32)
        for t, n in enumerate(tiles):
            ls = pl.ds(n * 128, 128)
            conv = jnp.concatenate(
                [o_ref[n, BLK * (NB - 1 - i) : BLK * (NB - i), :128] for i in range(NB)], axis=0
            )
            ds = flipped[:, t * 128 : (t + 1) * 128]
            kf, vf = k_ref[:, ls].astype(F32), v_ref[:, ls].astype(F32)
            qf, gf = q_ref[:, ls].astype(F32), g_ref[:, ls].astype(F32)
            skip = skip_ref[:, ls]
            conv = conv + skip * (kf * vf).astype(BF16).astype(F32)
            ds = ds + skip * dc_ref[0, n].astype(F32)
            mo_ref[:, ls] = (qf * conv).astype(BF16)
            qg_ref[:, ls] = (gf * conv).astype(BF16)
            kg_ref[:, ls] = (ds * vf).astype(BF16)
            vg_ref[:, ls] = (ds * kf).astype(BF16)
        for c in (p, p + HALF):
            for n in range(4):
                store(n, c).start()

    def arrive(p):
        c0, c1 = turn(0, p), turn(1, p)
        far(0, c0).wait_recv()

        @pl.when(d < 2)
        def _():
            x_ref[2, pl.ds(c0 * PER, PER)] = jnp.zeros((PER, ROWS, 128), BF16)

        @pl.when(core == 1)
        def _():
            near(0, c0, 2).start()

        far(1, c1).wait_recv()

        @pl.when(d >= n_ctx - 2)
        def _():
            dc_ref[2, pl.ds(c1 * PER, PER)] = jnp.zeros((PER, ROWS, 128), BF16)

        @pl.when(core == 0)
        def _():
            near(1, c1, 2).start()

    def complete(p):
        near(0, turn(0, p), 0).wait_recv()
        near(1, turn(1, p), 0).wait_recv()

    def stage1(step):
        other, ctx, ch = stage1_peer(step)
        return pltpu.make_async_remote_copy(
            src_ref=d1_ref.at[other], dst_ref=r1_ref.at[spot],
            send_sem=s1_send, recv_sem=s1_recv,
            device_id=(ctx, ch), device_id_type=MESH,
        )

    def stage2(step):
        other, ctx, ch = stage2_peer(step)
        return pltpu.make_async_remote_copy(
            src_ref=a1_ref.at[lax.div(other, 2)], dst_ref=r2_ref.at[e],
            send_sem=s2_send, recv_sem=s2_recv,
            device_id=(ctx, ch), device_id_type=MESH,
        )

    for n in range(2):
        pltpu.make_async_copy(m_ref.at[n], m_ref.at[n], mate_recv.at[n]).wait()
    filter_near(0)
    filter_near(1)
    for p in range(HALF):
        arrive(p)
        filter_terms(p)
        if p + 2 < HALF:
            filter_near(p + 2)
    for n in range(SHEET):
        rows = [d_ref[pl.ds(z * 8 * SHEET + 8 * n, 8)] for z in range(pile // 4)]
        d1_ref[n] = jnp.concatenate(rows, axis=0).astype(BF16)
    for step in range(1, SHEET):
        stage1(step).start()
    for p in range(HALF):
        complete(p)
    load_filt.wait()
    load_skip.wait()
    s_ref[:, :, : (NB - 1) * 128] = jnp.zeros((TILES, BLK, (NB - 1) * 128), BF16)
    s_ref[:, :, (NB - 1 + SPAN) * 128 :] = jnp.zeros((TILES, BLK, (NB - 1) * 128), BF16)
    tsh_ref[...] = jnp.zeros_like(tsh_ref)
    lax.fori_loop(0, TILES // 4, table, 0)
    arrive(4)
    lax.fori_loop(0, TILES // 4, own, 0)
    arrive(5)
    complete(4)
    rest(0)
    total = jnp.concatenate([d_ref[pl.ds(z * 8 * SHEET + 8 * spot, 8)] for z in range(pile // 4)], axis=0)
    others = r1_ref.at[pl.ds(0, SHEET - 1)]
    pltpu.make_async_copy(others, others, s1_recv).wait()
    for step in range(1, SHEET):
        total = total + r1_ref[stage1_peer(step)[0]].astype(F32)
    total = total * scale
    for n in range(pile // 2):
        a1_ref[n] = total[4 * n : 4 * n + 4]
    r2_ref[e] = a1_ref[lax.div(e, 2)]
    for step in range(1, pile):
        stage2(step).start()

    arrive(6)
    complete(5)
    rest(1)
    arrive(7)
    complete(6)
    rest(2)
    complete(7)
    rest(3)
    rest_of_pile = r2_ref.at[pl.ds(0, pile - 1)]
    pltpu.make_async_copy(rest_of_pile, rest_of_pile, s2_recv).wait()
    for hh in range(2):
        total = r2_ref[hh]
        for n in range(1, pile // 2):
            total = total + r2_ref[n * 2 + hh]
        fg_ref[:, hh * 128 : (hh + 1) * 128] = total

    last = pltpu.make_async_copy(fg_ref, fg_hbm, small_sem.at[0])
    last.start()

    for n, (src, dst) in enumerate(((mo_ref, mo_hbm), (qg_ref, qg_hbm), (kg_ref, kg_hbm), (vg_ref, vg_hbm))):
        pltpu.make_async_copy(src, dst, out_sem.at[n]).wait()
    for n in range(2):
        whole = (x_ref, dc_ref)[n].at[0]
        pltpu.make_async_copy(whole, whole, far_send.at[n]).wait()
        pltpu.make_async_copy(whole, whole, near_send.at[n]).wait()
        pltpu.make_async_copy(m_ref.at[n], m_ref.at[n], mate_send.at[n]).wait()
    pltpu.make_async_copy(others, others, s1_send).wait()
    pltpu.make_async_copy(rest_of_pile, rest_of_pile, s2_send).wait()
    last.wait()


def hand_over(*refs):
    src, dst, buf, small = refs[:5], refs[5:10], refs[10], refs[11]
    in_sem, out_sem = refs[12:]
    place = [buf.at[i] for i in range(4)] + [small]
    first = [pltpu.make_async_copy(src[i], place[i], in_sem.at[i]) for i in range(5)]
    then = [pltpu.make_async_copy(place[i], dst[i], out_sem.at[i // 4]) for i in range(5)]
    for copy in first:
        copy.start()
    for copy, onward in zip(first, then):
        copy.wait()
        onward.start()
    pltpu.make_async_copy(buf, buf, out_sem.at[0]).wait()
    then[4].wait()


def shards(q_proj, k_proj, v_proj, filt, skip, grad_out):
    n_ctx = lax.axis_size("ctx")
    scale = 1.0 / (16.0 * ROWS * n_ctx) ** 0.5
    hbm = pl.BlockSpec(memory_space=pltpu.HBM)
    big = jax.ShapeDtypeStruct((ROWS, LANES), BF16)
    results = (big, big, big, big, jax.ShapeDtypeStruct((4, 256), F32))
    pile = 2 * n_ctx // SHEET
    outs = pl.pallas_call(
        functools.partial(kernel, n_ctx, scale),
        out_shape=results,
        in_specs=[hbm] * 6,
        out_specs=(hbm,) * 5,
        scratch_shapes=[pltpu.VMEM((ROWS, LANES), BF16)] * 4
        + [
            pltpu.VMEM((TAPS, 128), F32),
            pltpu.VMEM((1, LANES), F32),
            pltpu.VMEM((3, TILES, ROWS, 128), BF16),
            pltpu.VMEM((3, TILES, ROWS, 128), BF16),
            pltpu.VMEM((2, TILES // 2, ROWS, 128), BF16),
            pltpu.VMEM((TILES, BLK, SLOTS * 128), BF16),
            pltpu.VMEM((TILES, ROWS, 256), F32),
            pltpu.VMEM((8, BLK, 128), BF16),
            pltpu.VMEM((4, 272, 128), F32),
            pltpu.VMEM((TILES, TAPS, 128), F32),
            pltpu.VMEM((4, 304, 128), F32),
            pltpu.VMEM((TAPS, 128), F32),
            pltpu.VMEM((SHEET, 2 * pile, 128), BF16),
            pltpu.VMEM((SHEET, 2 * pile, 128), BF16),
            pltpu.VMEM((pile // 2, 4, 128), F32),
            pltpu.VMEM((pile, 4, 128), F32),
        ]
        + [pltpu.VMEM((ROWS, LANES), BF16)] * 4
        + [
            pltpu.VMEM((4, 256), F32),
            pltpu.SemaphoreType.DMA((4, 3)),
            pltpu.SemaphoreType.DMA((4,)),
            pltpu.SemaphoreType.DMA((2,)),
            pltpu.SemaphoreType.DMA((2,)),
            pltpu.SemaphoreType.DMA((2, CHUNKS)),
            pltpu.SemaphoreType.DMA((2,)),
            pltpu.SemaphoreType.DMA((2, CHUNKS)),
            pltpu.SemaphoreType.DMA((2,)),
            pltpu.SemaphoreType.DMA((2,)),
            pltpu.SemaphoreType.DMA,
            pltpu.SemaphoreType.DMA,
            pltpu.SemaphoreType.DMA,
            pltpu.SemaphoreType.DMA,
        ],
        compiler_params=pltpu.CompilerParams(
            collective_id=0, has_side_effects=True, vmem_limit_bytes=60 * 1024 * 1024
        ),
        cost_estimate=pl.CostEstimate(flops=3 * 10**9, bytes_accessed=4 * 2**20, transcendentals=0),
        name="hyena",
    )(q_proj, k_proj, v_proj, filt, skip.reshape(1, LANES), grad_out)
    outs = pl.pallas_call(
        hand_over,
        out_shape=results,
        in_specs=[hbm] * 5,
        out_specs=(hbm,) * 5,
        scratch_shapes=[
            pltpu.VMEM((4, ROWS, LANES), BF16),
            pltpu.VMEM((4, 256), F32),
            pltpu.SemaphoreType.DMA((5,)),
            pltpu.SemaphoreType.DMA((2,)),
        ],
        compiler_params=pltpu.CompilerParams(vmem_limit_bytes=60 * 1024 * 1024),
        cost_estimate=pl.CostEstimate(flops=0, bytes_accessed=4 * 2**20, transcendentals=0),
        name="hand_over",
    )(*outs)
    return tuple(outs)


def solution(mesh):
    in_specs = (
        P("ctx", "ch"),
        P("ctx", "ch"),
        P("ctx", "ch"),
        P(None, "ch"),
        P("ch"),
        P("ctx", "ch"),
    )
    out_specs = (P("ctx", "ch"), P("ctx", "ch"), P("ctx", "ch"), P("ctx", "ch"), P("ctx", None))
    return jax.shard_map(shards, mesh=mesh, in_specs=in_specs, out_specs=out_specs, check_vma=False)
```

```python
import functools

import jax
import jax.numpy as jnp
from jax import lax
from jax.experimental import pallas as pl
from jax.experimental.pallas import tpu as pltpu
from jax.sharding import PartitionSpec as P

MESH = pl.DeviceIdType.MESH
F32 = jnp.float32
BF16 = jnp.bfloat16
ROWS = 128
LANES = 2048
TILES = LANES // 128
CHUNKS = 8
HALF = CHUNKS // 2
SHEET = 16
PER = TILES // CHUNKS
WIDTH = PER * 128
BLK = 16
NB = ROWS // BLK
TAPS = 256
SPAN = TAPS // BLK + 1
SLOTS = SPAN + 2 * (NB - 1)


def iota(shape, dim):
    return lax.broadcasted_iota(jnp.int32, shape, dim)


def kernel(
    n_ctx, scale,
    q_hbm, k_hbm, v_hbm, filt_hbm, skip_hbm, g_hbm,
    mo_hbm, qg_hbm, kg_hbm, vg_hbm, fg_hbm,
    q_ref, k_ref, v_ref, g_ref, filt_ref, skip_ref,
    x_ref, dc_ref, m_ref, s_ref, o_ref, mask_ref, sh_ref, z_ref, tsh_ref,
    d_ref, d1_ref, r1_ref, a1_ref, r2_ref,
    mo_ref, qg_ref, kg_ref, vg_ref, fg_ref,
    in_sem, out_sem, small_sem, far_send, far_recv, near_send, near_recv, mate_send, mate_recv,
    s1_send, s1_recv, s2_send, s2_recv,
):
    d = lax.axis_index("ctx")
    h = lax.axis_index("ch")
    up = lax.rem(d + 2, n_ctx)
    down = lax.rem(d + n_ctx - 2, n_ctx)
    core = lax.rem(d, 2)
    mate = d + 1 - 2 * core
    layer = lax.div(d, 2 * SHEET)
    spot = lax.rem(lax.div(d, 2), SHEET)
    pile = 2 * n_ctx // SHEET
    e = (layer * 2 + core) * 2 + h

    def turn(n, p):
        return (lax.rem(p + HALF, CHUNKS) if not isinstance(p, int) else (p + HALF) % CHUNKS) if n == 0 else p

    def load(n, part):
        src, dst = ((k_hbm, k_ref), (v_hbm, v_ref), (g_hbm, g_ref), (q_hbm, q_ref))[n]
        first, count = ((0, 1), (1, HALF - 1), (HALF, HALF))[part]
        cols = pl.ds(turn(n // 2, first) * WIDTH, count * WIDTH)
        return pltpu.make_async_copy(src.at[:, cols], dst.at[:, cols], in_sem.at[n, part])


    def stage1_peer(step):
        other = lax.rem(spot + step, SHEET)
        return other, (layer * SHEET + other) * 2 + core, h

    def stage2_peer(step):
        other = lax.rem(e + step, pile)
        ctx = (lax.div(other, 4) * SHEET + spot) * 2 + lax.rem(lax.div(other, 2), 2)
        return other, ctx, lax.rem(other, 2)

    barrier = pltpu.get_barrier_semaphore()
    peers = [(up, h), (down, h)]
    peers += [stage1_peer(step)[1:] for step in range(1, SHEET)]
    peers += [stage2_peer(step)[1:] for step in range(1, pile)]
    for peer in peers:
        pl.semaphore_signal(barrier, inc=1, device_id=peer, device_id_type=MESH)
    for n in range(4):
        load(n, 0).start()
    for part in range(1, 3):
        for n in range(4):
            load(n, part).start()
    load_filt = pltpu.make_async_copy(filt_hbm, filt_ref, small_sem.at[0])
    load_skip = pltpu.make_async_copy(skip_hbm, skip_ref, small_sem.at[1])
    load_filt.start()
    load_skip.start()

    flip = (iota((ROWS, ROWS), 0) + iota((ROWS, ROWS), 1) == ROWS - 1).astype(F32).astype(BF16)
    fr, fc = iota((ROWS, 2 * ROWS), 0), iota((ROWS, 2 * ROWS), 1) % ROWS
    flip2 = (jnp.logical_and(fr // BLK == fc // BLK, fr % BLK + fc % BLK == BLK - 1)).astype(F32).astype(BF16)
    for g in range(8):
        mask_ref[g] = (iota((BLK, 128), 1) // BLK == g).astype(F32).astype(BF16)

    def far(n, c):
        ref, target = ((x_ref, up), (dc_ref, down))[n]
        cs = pl.ds(c * PER, PER)
        return pltpu.make_async_remote_copy(
            src_ref=ref.at[0, cs], dst_ref=ref.at[2, cs],
            send_sem=far_send.at[n], recv_sem=far_recv.at[n, c],
            device_id=(target, h), device_id_type=MESH,
        )

    def near(n, c, src_slot):
        ref = (x_ref, dc_ref)[n]
        cs = pl.ds(c * PER, PER)
        return pltpu.make_async_remote_copy(
            src_ref=ref.at[src_slot, cs], dst_ref=ref.at[1, cs],
            send_sem=near_send.at[n], recv_sem=near_recv.at[n, c],
            device_id=(mate, h), device_id_type=MESH,
        )

    def gate(p):
        c0, c1 = turn(0, p), turn(1, p)
        if isinstance(p, int):
            for n in range(4):
                load(n, 0).wait()
        else:
            for part, first in ((1, 1), (2, HALF)):

                @pl.when(p == first)
                def _():
                    for n in range(4):
                        load(n, part).wait()

        cols = pl.ds(c0 * WIDTH if isinstance(p, int) else pl.multiple_of(c0 * WIDTH, WIDTH), WIDTH)
        st = (k_ref[:, cols].astype(F32) * v_ref[:, cols].astype(F32)).astype(BF16)
        st = jnp.dot(flip, st, preferred_element_type=F32).astype(BF16)
        for t in range(PER):
            x_ref[0, c0 * PER + t] = st[:, t * 128 : (t + 1) * 128]
        cols = pl.ds(c1 * WIDTH if isinstance(p, int) else pl.multiple_of(c1 * WIDTH, WIDTH), WIDTH)
        dc = (g_ref[:, cols].astype(F32) * q_ref[:, cols].astype(F32)).astype(BF16)
        for t in range(PER):
            dc_ref[0, c1 * PER + t] = dc[:, t * 128 : (t + 1) * 128]

    def to_mate(n, p):
        ref = (x_ref, dc_ref)[n]
        return pltpu.make_async_remote_copy(
            src_ref=ref.at[0, pl.ds(turn(n, p) * PER, PER)], dst_ref=m_ref.at[n, pl.ds((p - HALF) * PER, PER)],
            send_sem=mate_send.at[n], recv_sem=mate_recv.at[n],
            device_id=(mate, h), device_id_type=MESH,
        )

    def send(p):
        c0, c1 = turn(0, p), turn(1, p)
        far(0, c0).start()
        far(1, c1).start()
        if not isinstance(p, int):

            @pl.when(p >= HALF)
            def _():
                to_mate(0, p).start()
                to_mate(1, p).start()


        @pl.when(core == 0)
        def _():
            near(0, c0, 0).start()

        @pl.when(core == 1)
        def _():
            near(1, c1, 0).start()

    gate(0)
    pl.semaphore_wait(barrier, len(peers))
    send(0)
    def gate_step(p, carry):
        gate(p)
        send(p)
        return carry

    lax.fori_loop(1, CHUNKS, gate_step, 0)

    amt = 15 - iota((288, 128), 1) % BLK

    def table(c, carry):
        spots = iota((128, 512), 0) == 32 * c + iota((128, 512), 1) // BLK
        f = jnp.dot(filt_ref[...].astype(BF16), spots.astype(F32).astype(BF16), preferred_element_type=F32)
        edge = jnp.zeros((16, 128), F32)
        for t in range(4):
            z = jnp.concatenate([edge, f[:, t * 128 : (t + 1) * 128], edge], axis=0)
            for b in (8, 4, 2, 1):
                tsh_ref[t, 8:296] = z
                z = jnp.where((amt & b) != 0, tsh_ref[t, 8 - b : 296 - b], z)
            zb = z.astype(BF16)
            for u in range(SPAN):
                s_ref[c * 4 + t, :, (NB - 1 + u) * 128 : (NB + u) * 128] = zb[16 + 16 * u : 32 + 16 * u]
        return carry


    def spread(block):
        n_u = block.shape[0] // BLK
        wide = block.reshape(n_u, 1, BLK, 128) * mask_ref[...][None]
        return wide.reshape(n_u * 128, 128)

    def operator(n, u0, n_u):
        return jnp.concatenate(
            [s_ref[n, :, (NB - 1 - i + u0) * 128 : (NB - 1 - i + u0 + n_u) * 128] for i in range(NB)], axis=0
        )

    def own(c, carry):
        for t in range(4):
            n = c * 4 + t
            rhs = jnp.concatenate([spread(x_ref[0, n]), spread(dc_ref[0, n])], axis=1)
            o_ref[n] = jnp.dot(operator(n, 0, NB), rhs, preferred_element_type=F32)
        return carry

    amt2 = 15 - iota((264, 128), 1) % BLK
    even, odd = 1.0 - core.astype(F32), core.astype(F32)

    def filter_tiles(p):
        tiles = [(p * PER + t, dc_ref, x_ref, 0, even) for t in range(PER)]
        return tiles + [((p + HALF) * PER + t, x_ref, dc_ref, 1, odd) for t in range(PER)]

    def correlate(block, n, short, side):
        pad = jnp.zeros(((NB - 1) * BLK, 128), BF16)
        rows = jnp.concatenate([pad, block, pad], axis=0)
        lhs = jnp.concatenate([rows[BLK * i : BLK * i + (2 * NB - 1) * BLK] for i in range(NB)], axis=1)
        both = (spread(short[0, n]), spread(m_ref[side, n - side * HALF * PER]))
        rhs = [jnp.concatenate([b[(NB - 1 - i) * 128 : (NB - i) * 128] for i in range(NB)], axis=1) for b in both]
        rhs = jnp.concatenate(rhs, axis=0)
        return lax.dot_general(lhs, rhs, (((1,), (1,)), ((), ())), preferred_element_type=F32)

    def filter_near(p):
        for n, long, short, side, far_weight in filter_tiles(p):
            y = correlate(long[0, n], n, short, side)
            z_ref[n, 0:16] = y[112:128, :128]
            z_ref[n, 16:128] = y[128:240, :128] + (1.0 - far_weight) * y[0:112, 128:]
            z_ref[n, 128:256] = (1.0 - far_weight) * y[112:240, 128:]

    def filter_terms(p):
        tiles = filter_tiles(p)
        parts, spots = [], []
        for t, (n, long, short, side, far_weight) in enumerate(tiles):
            y = correlate(long[2, n], n, short, side)
            sh_ref[t, 0:16] = z_ref[n, 0:16]
            sh_ref[t, 16:144] = z_ref[n, 16:144] + far_weight * y[0:128, 128:]
            sh_ref[t, 144:256] = z_ref[n, 144:256] + far_weight * y[128:240, 128:] + y[0:112, :128]
            sh_ref[t, 256:272] = y[112:128, :128]
        for t, (n, long, short, side, far_weight) in enumerate(tiles):
            z = jnp.where((amt2 & 8) != 0, sh_ref[t, 8:272], sh_ref[t, 0:264])
            for b in (4, 2, 1):
                sh_ref[t, 0:264] = z
                z = jnp.where((amt2 & b) != 0, sh_ref[t, b : 264 + b], z)
            z = z[:TAPS]
            hi = z.astype(BF16)
            parts += [hi, (z - hi.astype(F32)).astype(BF16)]
            spot = (iota((256, 128), 1) == 8 * n + iota((256, 128), 0) % 128 // BLK).astype(F32)
            spots.append(spot.astype(BF16))
        terms = jnp.dot(
            jnp.concatenate(parts, axis=1), jnp.concatenate(spots, axis=0), preferred_element_type=F32
        )
        d_ref[...] += terms

    def store(n, c):
        src, dst = ((mo_ref, mo_hbm), (qg_ref, qg_hbm), (kg_ref, kg_hbm), (vg_ref, vg_hbm))[n]
        cols = pl.ds(c * WIDTH if isinstance(c, int) else pl.multiple_of(c * WIDTH, WIDTH), WIDTH)
        return pltpu.make_async_copy(src.at[:, cols], dst.at[:, cols], out_sem.at[n])

    def rest(p):
        tiles = [p * PER + t for t in range(PER)] + [(p + HALF) * PER + t for t in range(PER)]
        his, los = [], []
        for n in tiles:
            rx = jnp.concatenate([spread(x_ref[1, n]), spread(x_ref[2, n])], axis=0)
            rd = jnp.concatenate([spread(dc_ref[1, n]), spread(dc_ref[2, n])], axis=0)
            out = o_ref[n] + jnp.dot(
                operator(n, NB, 2 * NB), jnp.concatenate([rx, rd], axis=1), preferred_element_type=F32
            )
            o_ref[n] = out
            ds = out[:, 128:]
            hi = ds.astype(BF16)
            his.append(hi)
            los.append((ds - hi.astype(F32)).astype(BF16))
        pair = jnp.concatenate([jnp.concatenate(his, axis=1), jnp.concatenate(los, axis=1)], axis=0)
        flipped = jnp.dot(flip2, pair, preferred_element_type=F32)
        for t, n in enumerate(tiles):
            ls = pl.ds(n * 128 if isinstance(n, int) else pl.multiple_of(n * 128, 128), 128)
            conv = jnp.concatenate(
                [o_ref[n, BLK * (NB - 1 - i) : BLK * (NB - i), :128] for i in range(NB)], axis=0
            )
            ds = flipped[:, t * 128 : (t + 1) * 128]
            kf, vf = k_ref[:, ls].astype(F32), v_ref[:, ls].astype(F32)
            qf, gf = q_ref[:, ls].astype(F32), g_ref[:, ls].astype(F32)
            skip = skip_ref[:, ls]
            conv = conv + skip * (kf * vf).astype(BF16).astype(F32)
            ds = ds + skip * dc_ref[0, n].astype(F32)
            mo_ref[:, ls] = (qf * conv).astype(BF16)
            qg_ref[:, ls] = (gf * conv).astype(BF16)
            kg_ref[:, ls] = (ds * vf).astype(BF16)
            vg_ref[:, ls] = (ds * kf).astype(BF16)
        for c in (p, p + HALF):
            for n in range(4):
                store(n, c).start()

    def arrive(p):
        c0, c1 = turn(0, p), turn(1, p)
        far(0, c0).wait_recv()

        @pl.when(d < 2)
        def _():
            x_ref[2, pl.ds(c0 * PER, PER)] = jnp.zeros((PER, ROWS, 128), BF16)

        @pl.when(core == 1)
        def _():
            near(0, c0, 2).start()

        far(1, c1).wait_recv()

        @pl.when(d >= n_ctx - 2)
        def _():
            dc_ref[2, pl.ds(c1 * PER, PER)] = jnp.zeros((PER, ROWS, 128), BF16)

        @pl.when(core == 0)
        def _():
            near(1, c1, 2).start()

    def complete(p):
        near(0, turn(0, p), 0).wait_recv()
        near(1, turn(1, p), 0).wait_recv()

    def stage1(step):
        other, ctx, ch = stage1_peer(step)
        return pltpu.make_async_remote_copy(
            src_ref=d1_ref.at[other], dst_ref=r1_ref.at[spot],
            send_sem=s1_send, recv_sem=s1_recv,
            device_id=(ctx, ch), device_id_type=MESH,
        )

    def stage2(step):
        other, ctx, ch = stage2_peer(step)
        return pltpu.make_async_remote_copy(
            src_ref=a1_ref.at[lax.div(other, 2)], dst_ref=r2_ref.at[e],
            send_sem=s2_send, recv_sem=s2_recv,
            device_id=(ctx, ch), device_id_type=MESH,
        )

    for n in range(2):
        pltpu.make_async_copy(m_ref.at[n], m_ref.at[n], mate_recv.at[n]).wait()
    def near_step(p, carry):
        filter_near(p)
        return carry

    def far_step(p, carry):
        arrive(p)
        filter_terms(p)
        return carry

    d_ref[...] = jnp.zeros_like(d_ref)
    lax.fori_loop(0, HALF, near_step, 0)
    lax.fori_loop(0, HALF, far_step, 0)
    for n in range(SHEET):
        rows = [d_ref[pl.ds(z * 8 * SHEET + 8 * n, 8)] for z in range(pile // 4)]
        d1_ref[n] = jnp.concatenate(rows, axis=0)
    for step in range(1, SHEET):
        stage1(step).start()
    for p in range(HALF):
        complete(p)
    load_filt.wait()
    load_skip.wait()
    s_ref[:, :, : (NB - 1) * 128] = jnp.zeros((TILES, BLK, (NB - 1) * 128), BF16)
    s_ref[:, :, (NB - 1 + SPAN) * 128 :] = jnp.zeros((TILES, BLK, (NB - 1) * 128), BF16)
    tsh_ref[...] = jnp.zeros_like(tsh_ref)
    lax.fori_loop(0, TILES // 4, table, 0)
    arrive(4)
    lax.fori_loop(0, TILES // 4, own, 0)
    arrive(5)
    complete(4)
    rest(0)
    total = jnp.concatenate([d_ref[pl.ds(z * 8 * SHEET + 8 * spot, 8)] for z in range(pile // 4)], axis=0)
    others = r1_ref.at[pl.ds(0, SHEET - 1)]
    pltpu.make_async_copy(others, others, s1_recv).wait()
    for step in range(1, SHEET):
        total = total + r1_ref[stage1_peer(step)[0]]
    total = total * scale
    for n in range(pile // 2):
        a1_ref[n] = total[4 * n : 4 * n + 4]
    r2_ref[e] = a1_ref[lax.div(e, 2)]
    for step in range(1, pile):
        stage2(step).start()

    def rest_step(p, carry):
        @pl.when(p + 1 < HALF)
        def _():
            arrive(p + HALF + 1)

        complete(p + HALF)
        rest(p)
        return carry

    lax.fori_loop(1, HALF, rest_step, 0)
    rest_of_pile = r2_ref.at[pl.ds(0, pile - 1)]
    pltpu.make_async_copy(rest_of_pile, rest_of_pile, s2_recv).wait()
    for hh in range(2):
        total = r2_ref[hh]
        for n in range(1, pile // 2):
            total = total + r2_ref[n * 2 + hh]
        fg_ref[:, hh * 128 : (hh + 1) * 128] = total

    last = pltpu.make_async_copy(fg_ref, fg_hbm, small_sem.at[0])
    last.start()

    for n, (src, dst) in enumerate(((mo_ref, mo_hbm), (qg_ref, qg_hbm), (kg_ref, kg_hbm), (vg_ref, vg_hbm))):
        pltpu.make_async_copy(src, dst, out_sem.at[n]).wait()
    for n in range(2):
        whole = (x_ref, dc_ref)[n].at[0]
        pltpu.make_async_copy(whole, whole, far_send.at[n]).wait()
        pltpu.make_async_copy(whole, whole, near_send.at[n]).wait()
        pltpu.make_async_copy(m_ref.at[n], m_ref.at[n], mate_send.at[n]).wait()
    pltpu.make_async_copy(others, others, s1_send).wait()
    pltpu.make_async_copy(rest_of_pile, rest_of_pile, s2_send).wait()
    last.wait()


def hand_over(*refs):
    src, dst, buf, small = refs[:5], refs[5:10], refs[10], refs[11]
    in_sem, out_sem = refs[12:]
    place = [buf.at[i] for i in range(4)] + [small]
    first = [pltpu.make_async_copy(src[i], place[i], in_sem.at[i]) for i in range(5)]
    then = [pltpu.make_async_copy(place[i], dst[i], out_sem.at[i // 4]) for i in range(5)]
    for copy in first:
        copy.start()
    for copy, onward in zip(first, then):
        copy.wait()
        onward.start()
    pltpu.make_async_copy(buf, buf, out_sem.at[0]).wait()
    then[4].wait()


def shards(q_proj, k_proj, v_proj, filt, skip, grad_out):
    n_ctx = lax.axis_size("ctx")
    scale = 1.0 / (16.0 * ROWS * n_ctx) ** 0.5
    hbm = pl.BlockSpec(memory_space=pltpu.HBM)
    big = jax.ShapeDtypeStruct((ROWS, LANES), BF16)
    results = (big, big, big, big, jax.ShapeDtypeStruct((4, 256), F32))
    pile = 2 * n_ctx // SHEET
    outs = pl.pallas_call(
        functools.partial(kernel, n_ctx, scale),
        out_shape=results,
        in_specs=[hbm] * 6,
        out_specs=(hbm,) * 5,
        scratch_shapes=[pltpu.VMEM((ROWS, LANES), BF16)] * 4
        + [
            pltpu.VMEM((TAPS, 128), F32),
            pltpu.VMEM((1, LANES), F32),
            pltpu.VMEM((3, TILES, ROWS, 128), BF16),
            pltpu.VMEM((3, TILES, ROWS, 128), BF16),
            pltpu.VMEM((2, TILES // 2, ROWS, 128), BF16),
            pltpu.VMEM((TILES, BLK, SLOTS * 128), BF16),
            pltpu.VMEM((TILES, ROWS, 256), F32),
            pltpu.VMEM((8, BLK, 128), BF16),
            pltpu.VMEM((4, 272, 128), F32),
            pltpu.VMEM((TILES, TAPS, 128), F32),
            pltpu.VMEM((4, 304, 128), F32),
            pltpu.VMEM((TAPS, 128), F32),
            pltpu.VMEM((SHEET, 2 * pile, 128), F32),
            pltpu.VMEM((SHEET, 2 * pile, 128), F32),
            pltpu.VMEM((pile // 2, 4, 128), F32),
            pltpu.VMEM((pile, 4, 128), F32),
        ]
        + [pltpu.VMEM((ROWS, LANES), BF16)] * 4
        + [
            pltpu.VMEM((4, 256), F32),
            pltpu.SemaphoreType.DMA((4, 3)),
            pltpu.SemaphoreType.DMA((4,)),
            pltpu.SemaphoreType.DMA((2,)),
            pltpu.SemaphoreType.DMA((2,)),
            pltpu.SemaphoreType.DMA((2, CHUNKS)),
            pltpu.SemaphoreType.DMA((2,)),
            pltpu.SemaphoreType.DMA((2, CHUNKS)),
            pltpu.SemaphoreType.DMA((2,)),
            pltpu.SemaphoreType.DMA((2,)),
            pltpu.SemaphoreType.DMA,
            pltpu.SemaphoreType.DMA,
            pltpu.SemaphoreType.DMA,
            pltpu.SemaphoreType.DMA,
        ],
        compiler_params=pltpu.CompilerParams(
            collective_id=0, has_side_effects=True, vmem_limit_bytes=60 * 1024 * 1024
        ),
        cost_estimate=pl.CostEstimate(flops=3 * 10**9, bytes_accessed=4 * 2**20, transcendentals=0),
        name="hyena",
    )(q_proj, k_proj, v_proj, filt, skip.reshape(1, LANES), grad_out)
    outs = pl.pallas_call(
        hand_over,
        out_shape=results,
        in_specs=[hbm] * 5,
        out_specs=(hbm,) * 5,
        scratch_shapes=[
            pltpu.VMEM((4, ROWS, LANES), BF16),
            pltpu.VMEM((4, 256), F32),
            pltpu.SemaphoreType.DMA((5,)),
            pltpu.SemaphoreType.DMA((2,)),
        ],
        compiler_params=pltpu.CompilerParams(vmem_limit_bytes=60 * 1024 * 1024),
        cost_estimate=pl.CostEstimate(flops=0, bytes_accessed=4 * 2**20, transcendentals=0),
        name="hand_over",
    )(*outs)
    return tuple(outs)


def solution(mesh):
    in_specs = (
        P("ctx", "ch"),
        P("ctx", "ch"),
        P("ctx", "ch"),
        P(None, "ch"),
        P("ch"),
        P("ctx", "ch"),
    )
    out_specs = (P("ctx", "ch"), P("ctx", "ch"), P("ctx", "ch"), P("ctx", "ch"), P("ctx", None))
    return jax.shard_map(shards, mesh=mesh, in_specs=in_specs, out_specs=out_specs, check_vma=False)
```

```python
import functools

import jax
import jax.numpy as jnp
from jax import lax
from jax.experimental import pallas as pl
from jax.experimental.pallas import tpu as pltpu
from jax.sharding import PartitionSpec as P

MESH = pl.DeviceIdType.MESH
F32 = jnp.float32
BF16 = jnp.bfloat16
ROWS = 128
LANES = 2048
TILES = LANES // 128
CHUNKS = 8
HALF = CHUNKS // 2
SHEET = 16
PER = TILES // CHUNKS
WIDTH = PER * 128
BLK = 16
NB = ROWS // BLK
TAPS = 256
SPAN = TAPS // BLK + 1
SLOTS = SPAN + 2 * (NB - 1)


def iota(shape, dim):
    return lax.broadcasted_iota(jnp.int32, shape, dim)


def kernel(
    n_ctx, scale,
    q_hbm, k_hbm, v_hbm, filt_hbm, skip_hbm, g_hbm,
    mo_hbm, qg_hbm, kg_hbm, vg_hbm, fg_hbm,
    q_ref, k_ref, v_ref, g_ref, filt_ref, skip_ref,
    x_ref, dc_ref, m_ref, s_ref, o_ref, mask_ref, sh_ref, z_ref, tsh_ref,
    d_ref, d1_ref, r1_ref, a1_ref, r2_ref,
    mo_ref, qg_ref, kg_ref, vg_ref, fg_ref,
    in_sem, out_sem, small_sem, far_send, far_recv, near_send, near_recv, mate_send, mate_recv,
    s1_send, s1_recv, s2_send, s2_recv,
):
    d = lax.axis_index("ctx")
    h = lax.axis_index("ch")
    up = lax.rem(d + 2, n_ctx)
    down = lax.rem(d + n_ctx - 2, n_ctx)
    core = lax.rem(d, 2)
    mate = d + 1 - 2 * core
    layer = lax.div(d, 2 * SHEET)
    spot = lax.rem(lax.div(d, 2), SHEET)
    pile = 2 * n_ctx // SHEET
    e = (layer * 2 + core) * 2 + h

    def turn(n, p):
        return (lax.rem(p + HALF, CHUNKS) if not isinstance(p, int) else (p + HALF) % CHUNKS) if n == 0 else p

    def load(n, part):
        src, dst = ((k_hbm, k_ref), (v_hbm, v_ref), (g_hbm, g_ref), (q_hbm, q_ref))[n]
        first, count = ((0, 1), (1, HALF - 1), (HALF, HALF))[part]
        cols = pl.ds(turn(n // 2, first) * WIDTH, count * WIDTH)
        return pltpu.make_async_copy(src.at[:, cols], dst.at[:, cols], in_sem.at[n, part])


    def stage1_peer(step):
        other = lax.rem(spot + step, SHEET)
        return other, (layer * SHEET + other) * 2 + core, h

    def stage2_peer(step):
        other = lax.rem(e + step, pile)
        ctx = (lax.div(other, 4) * SHEET + spot) * 2 + lax.rem(lax.div(other, 2), 2)
        return other, ctx, lax.rem(other, 2)

    barrier = pltpu.get_barrier_semaphore()
    peers = [(up, h), (down, h)]
    peers += [stage1_peer(step)[1:] for step in range(1, SHEET)]
    peers += [stage2_peer(step)[1:] for step in range(1, pile)]
    for peer in peers:
        pl.semaphore_signal(barrier, inc=1, device_id=peer, device_id_type=MESH)
    for n in range(4):
        load(n, 0).start()
    for part in range(1, 3):
        for n in range(4):
            load(n, part).start()
    load_filt = pltpu.make_async_copy(filt_hbm, filt_ref, small_sem.at[0])
    load_skip = pltpu.make_async_copy(skip_hbm, skip_ref, small_sem.at[1])
    load_filt.start()
    load_skip.start()

    flip = (iota((ROWS, ROWS), 0) + iota((ROWS, ROWS), 1) == ROWS - 1).astype(F32).astype(BF16)
    fr, fc = iota((ROWS, 2 * ROWS), 0), iota((ROWS, 2 * ROWS), 1) % ROWS
    flip2 = (jnp.logical_and(fr // BLK == fc // BLK, fr % BLK + fc % BLK == BLK - 1)).astype(F32).astype(BF16)
    for g in range(8):
        mask_ref[g] = (iota((BLK, 128), 1) // BLK == g).astype(F32).astype(BF16)

    def far(n, c):
        ref, target = ((x_ref, up), (dc_ref, down))[n]
        cs = pl.ds(c * PER, PER)
        return pltpu.make_async_remote_copy(
            src_ref=ref.at[0, cs], dst_ref=ref.at[2, cs],
            send_sem=far_send.at[n], recv_sem=far_recv.at[n, c],
            device_id=(target, h), device_id_type=MESH,
        )

    def near(n, c, src_slot):
        ref = (x_ref, dc_ref)[n]
        cs = pl.ds(c * PER, PER)
        return pltpu.make_async_remote_copy(
            src_ref=ref.at[src_slot, cs], dst_ref=ref.at[1, cs],
            send_sem=near_send.at[n], recv_sem=near_recv.at[n, lax.rem(c, HALF)],
            device_id=(mate, h), device_id_type=MESH,
        )

    def gate(p):
        c0, c1 = turn(0, p), turn(1, p)
        if isinstance(p, int):
            for n in range(4):
                load(n, 0).wait()
        else:
            for part, first in ((1, 1), (2, HALF)):

                @pl.when(p == first)
                def _():
                    for n in range(4):
                        load(n, part).wait()

        cols = pl.ds(c0 * WIDTH if isinstance(p, int) else pl.multiple_of(c0 * WIDTH, WIDTH), WIDTH)
        st = (k_ref[:, cols].astype(F32) * v_ref[:, cols].astype(F32)).astype(BF16)
        st = jnp.dot(flip, st, preferred_element_type=F32).astype(BF16)
        for t in range(PER):
            x_ref[0, c0 * PER + t] = st[:, t * 128 : (t + 1) * 128]
        cols = pl.ds(c1 * WIDTH if isinstance(p, int) else pl.multiple_of(c1 * WIDTH, WIDTH), WIDTH)
        dc = (g_ref[:, cols].astype(F32) * q_ref[:, cols].astype(F32)).astype(BF16)
        for t in range(PER):
            dc_ref[0, c1 * PER + t] = dc[:, t * 128 : (t + 1) * 128]

    def to_mate(n, p):
        ref = (x_ref, dc_ref)[n]
        return pltpu.make_async_remote_copy(
            src_ref=ref.at[0, pl.ds(turn(n, p) * PER, PER)], dst_ref=m_ref.at[n, pl.ds((p - HALF) * PER, PER)],
            send_sem=mate_send.at[n], recv_sem=mate_recv.at[n],
            device_id=(mate, h), device_id_type=MESH,
        )

    def send(p):
        c0, c1 = turn(0, p), turn(1, p)
        far(0, c0).start()
        far(1, c1).start()
        if not isinstance(p, int):

            @pl.when(p >= HALF)
            def _():
                to_mate(0, p).start()
                to_mate(1, p).start()


        @pl.when(core == 0)
        def _():
            near(0, c0, 0).start()

        @pl.when(core == 1)
        def _():
            near(1, c1, 0).start()

    gate(0)
    pl.semaphore_wait(barrier, len(peers))
    send(0)
    def gate_step(p, carry):
        gate(p)
        send(p)
        return carry

    lax.fori_loop(1, CHUNKS, gate_step, 0)

    amt = 15 - iota((288, 128), 1) % BLK

    def table(c, carry):
        spots = iota((128, 512), 0) == 32 * c + iota((128, 512), 1) // BLK
        f = jnp.dot(filt_ref[...].astype(BF16), spots.astype(F32).astype(BF16), preferred_element_type=F32)
        edge = jnp.zeros((16, 128), F32)
        for t in range(4):
            z = jnp.concatenate([edge, f[:, t * 128 : (t + 1) * 128], edge], axis=0)
            for b in (8, 4, 2, 1):
                tsh_ref[t, 8:296] = z
                z = jnp.where((amt & b) != 0, tsh_ref[t, 8 - b : 296 - b], z)
            zb = z.astype(BF16)
            for u in range(SPAN):
                s_ref[c * 4 + t, :, (NB - 1 + u) * 128 : (NB + u) * 128] = zb[16 + 16 * u : 32 + 16 * u]
        return carry


    def spread(block):
        n_u = block.shape[0] // BLK
        wide = block.reshape(n_u, 1, BLK, 128) * mask_ref[...][None]
        return wide.reshape(n_u * 128, 128)

    def operator(n, u0, n_u):
        return jnp.concatenate(
            [s_ref[n, :, (NB - 1 - i + u0) * 128 : (NB - 1 - i + u0 + n_u) * 128] for i in range(NB)], axis=0
        )

    def own(c, carry):
        for t in range(4):
            n = c * 4 + t
            rhs = jnp.concatenate([spread(x_ref[0, n]), spread(dc_ref[0, n])], axis=1)
            o_ref[n] = jnp.dot(operator(n, 0, NB), rhs, preferred_element_type=F32)
        return carry

    amt2 = 15 - iota((264, 128), 1) % BLK
    even, odd = 1.0 - core.astype(F32), core.astype(F32)

    def filter_tiles(p):
        tiles = [(p * PER + t, dc_ref, x_ref, 0, even) for t in range(PER)]
        return tiles + [((p + HALF) * PER + t, x_ref, dc_ref, 1, odd) for t in range(PER)]

    def correlate(block, n, short, side):
        pad = jnp.zeros(((NB - 1) * BLK, 128), BF16)
        rows = jnp.concatenate([pad, block, pad], axis=0)
        lhs = jnp.concatenate([rows[BLK * i : BLK * i + (2 * NB - 1) * BLK] for i in range(NB)], axis=1)
        both = (spread(short[0, n]), spread(m_ref[side, n - side * HALF * PER]))
        rhs = [jnp.concatenate([b[(NB - 1 - i) * 128 : (NB - i) * 128] for i in range(NB)], axis=1) for b in both]
        rhs = jnp.concatenate(rhs, axis=0)
        return lax.dot_general(lhs, rhs, (((1,), (1,)), ((), ())), preferred_element_type=F32)

    def filter_near(p):
        for n, long, short, side, far_weight in filter_tiles(p):
            y = correlate(long[0, n], n, short, side)
            z_ref[n, 0:16] = y[112:128, :128]
            z_ref[n, 16:128] = y[128:240, :128] + (1.0 - far_weight) * y[0:112, 128:]
            z_ref[n, 128:256] = (1.0 - far_weight) * y[112:240, 128:]

    def filter_terms(p):
        tiles = filter_tiles(p)
        parts, spots = [], []
        for t, (n, long, short, side, far_weight) in enumerate(tiles):
            y = correlate(long[2, n], n, short, side)
            sh_ref[t, 0:16] = z_ref[n, 0:16]
            sh_ref[t, 16:144] = z_ref[n, 16:144] + far_weight * y[0:128, 128:]
            sh_ref[t, 144:256] = z_ref[n, 144:256] + far_weight * y[128:240, 128:] + y[0:112, :128]
            sh_ref[t, 256:272] = y[112:128, :128]
        for t, (n, long, short, side, far_weight) in enumerate(tiles):
            z = jnp.where((amt2 & 8) != 0, sh_ref[t, 8:272], sh_ref[t, 0:264])
            for b in (4, 2, 1):
                sh_ref[t, 0:264] = z
                z = jnp.where((amt2 & b) != 0, sh_ref[t, b : 264 + b], z)
            z = z[:TAPS]
            hi = z.astype(BF16)
            parts += [hi, (z - hi.astype(F32)).astype(BF16)]
            spot = (iota((256, 128), 1) == 8 * n + iota((256, 128), 0) % 128 // BLK).astype(F32)
            spots.append(spot.astype(BF16))
        terms = jnp.dot(
            jnp.concatenate(parts, axis=1), jnp.concatenate(spots, axis=0), preferred_element_type=F32
        )
        d_ref[...] += terms

    def store(n, c):
        src, dst = ((mo_ref, mo_hbm), (qg_ref, qg_hbm), (kg_ref, kg_hbm), (vg_ref, vg_hbm))[n]
        cols = pl.ds(c * WIDTH if isinstance(c, int) else pl.multiple_of(c * WIDTH, WIDTH), WIDTH)
        return pltpu.make_async_copy(src.at[:, cols], dst.at[:, cols], out_sem.at[n])

    def rest(p):
        tiles = [p * PER + t for t in range(PER)] + [(p + HALF) * PER + t for t in range(PER)]
        his, los = [], []
        for n in tiles:
            rx = jnp.concatenate([spread(x_ref[1, n]), spread(x_ref[2, n])], axis=0)
            rd = jnp.concatenate([spread(dc_ref[1, n]), spread(dc_ref[2, n])], axis=0)
            out = o_ref[n] + jnp.dot(
                operator(n, NB, 2 * NB), jnp.concatenate([rx, rd], axis=1), preferred_element_type=F32
            )
            o_ref[n] = out
            ds = out[:, 128:]
            hi = ds.astype(BF16)
            his.append(hi)
            los.append((ds - hi.astype(F32)).astype(BF16))
        pair = jnp.concatenate([jnp.concatenate(his, axis=1), jnp.concatenate(los, axis=1)], axis=0)
        flipped = jnp.dot(flip2, pair, preferred_element_type=F32)
        for t, n in enumerate(tiles):
            ls = pl.ds(n * 128 if isinstance(n, int) else pl.multiple_of(n * 128, 128), 128)
            conv = jnp.concatenate(
                [o_ref[n, BLK * (NB - 1 - i) : BLK * (NB - i), :128] for i in range(NB)], axis=0
            )
            ds = flipped[:, t * 128 : (t + 1) * 128]
            kf, vf = k_ref[:, ls].astype(F32), v_ref[:, ls].astype(F32)
            qf, gf = q_ref[:, ls].astype(F32), g_ref[:, ls].astype(F32)
            skip = skip_ref[:, ls]
            conv = conv + skip * (kf * vf).astype(BF16).astype(F32)
            ds = ds + skip * dc_ref[0, n].astype(F32)
            mo_ref[:, ls] = (qf * conv).astype(BF16)
            qg_ref[:, ls] = (gf * conv).astype(BF16)
            kg_ref[:, ls] = (ds * vf).astype(BF16)
            vg_ref[:, ls] = (ds * kf).astype(BF16)
        for c in (p, p + HALF):
            for n in range(4):
                store(n, c).start()

    def arrive(p):
        c0, c1 = turn(0, p), turn(1, p)
        far(0, c0).wait_recv()

        @pl.when(d < 2)
        def _():
            x_ref[2, pl.ds(c0 * PER, PER)] = jnp.zeros((PER, ROWS, 128), BF16)

        @pl.when(core == 1)
        def _():
            near(0, c0, 2).start()

        far(1, c1).wait_recv()

        @pl.when(d >= n_ctx - 2)
        def _():
            dc_ref[2, pl.ds(c1 * PER, PER)] = jnp.zeros((PER, ROWS, 128), BF16)

        @pl.when(core == 0)
        def _():
            near(1, c1, 2).start()

    def complete(p):
        for n in range(2):
            two = (x_ref, dc_ref)[n].at[1, pl.ds(0, 2 * PER)]
            pltpu.make_async_copy(two, two, near_recv.at[n, p]).wait()

    def stage1(step):
        other, ctx, ch = stage1_peer(step)
        return pltpu.make_async_remote_copy(
            src_ref=d1_ref.at[other], dst_ref=r1_ref.at[spot],
            send_sem=s1_send, recv_sem=s1_recv,
            device_id=(ctx, ch), device_id_type=MESH,
        )

    def stage2(step):
        other, ctx, ch = stage2_peer(step)
        return pltpu.make_async_remote_copy(
            src_ref=a1_ref.at[lax.div(other, 2)], dst_ref=r2_ref.at[e],
            send_sem=s2_send, recv_sem=s2_recv,
            device_id=(ctx, ch), device_id_type=MESH,
        )

    for n in range(2):
        pltpu.make_async_copy(m_ref.at[n], m_ref.at[n], mate_recv.at[n]).wait()
    def near_step(p, carry):
        filter_near(p)
        return carry

    def far_step(p, carry):
        arrive(p)
        filter_terms(p)
        return carry

    d_ref[...] = jnp.zeros_like(d_ref)
    lax.fori_loop(0, HALF, near_step, 0)
    lax.fori_loop(0, HALF, far_step, 0)
    for n in range(SHEET):
        rows = [d_ref[pl.ds(z * 8 * SHEET + 8 * n, 8)] for z in range(pile // 4)]
        d1_ref[n] = jnp.concatenate(rows, axis=0)
    for step in range(1, SHEET):
        stage1(step).start()
    load_filt.wait()
    load_skip.wait()
    s_ref[:, :, : (NB - 1) * 128] = jnp.zeros((TILES, BLK, (NB - 1) * 128), BF16)
    s_ref[:, :, (NB - 1 + SPAN) * 128 :] = jnp.zeros((TILES, BLK, (NB - 1) * 128), BF16)
    tsh_ref[...] = jnp.zeros_like(tsh_ref)
    lax.fori_loop(0, TILES // 4, table, 0)
    arrive(4)
    lax.fori_loop(0, TILES // 4, own, 0)
    arrive(5)
    complete(0)
    rest(0)
    total = jnp.concatenate([d_ref[pl.ds(z * 8 * SHEET + 8 * spot, 8)] for z in range(pile // 4)], axis=0)
    others = r1_ref.at[pl.ds(0, SHEET - 1)]
    pltpu.make_async_copy(others, others, s1_recv).wait()
    for step in range(1, SHEET):
        total = total + r1_ref[stage1_peer(step)[0]]
    total = total * scale
    for n in range(pile // 2):
        a1_ref[n] = total[4 * n : 4 * n + 4]
    r2_ref[e] = a1_ref[lax.div(e, 2)]
    for step in range(1, pile):
        stage2(step).start()

    def rest_step(p, carry):
        @pl.when(p + 1 < HALF)
        def _():
            arrive(p + HALF + 1)

        complete(p)
        rest(p)
        return carry

    lax.fori_loop(1, HALF, rest_step, 0)
    rest_of_pile = r2_ref.at[pl.ds(0, pile - 1)]
    pltpu.make_async_copy(rest_of_pile, rest_of_pile, s2_recv).wait()
    for hh in range(2):
        total = r2_ref[hh]
        for n in range(1, pile // 2):
            total = total + r2_ref[n * 2 + hh]
        fg_ref[:, hh * 128 : (hh + 1) * 128] = total

    last = pltpu.make_async_copy(fg_ref, fg_hbm, small_sem.at[0])
    last.start()

    for n, (src, dst) in enumerate(((mo_ref, mo_hbm), (qg_ref, qg_hbm), (kg_ref, kg_hbm), (vg_ref, vg_hbm))):
        pltpu.make_async_copy(src, dst, out_sem.at[n]).wait()
    for n in range(2):
        whole = (x_ref, dc_ref)[n].at[0]
        pltpu.make_async_copy(whole, whole, far_send.at[n]).wait()
        pltpu.make_async_copy(whole, whole, near_send.at[n]).wait()
        pltpu.make_async_copy(m_ref.at[n], m_ref.at[n], mate_send.at[n]).wait()
    pltpu.make_async_copy(others, others, s1_send).wait()
    pltpu.make_async_copy(rest_of_pile, rest_of_pile, s2_send).wait()
    last.wait()


def hand_over(*refs):
    src, dst, buf, small = refs[:5], refs[5:10], refs[10], refs[11]
    in_sem, out_sem = refs[12:]
    place = [buf.at[i] for i in range(4)] + [small]
    first = [pltpu.make_async_copy(src[i], place[i], in_sem.at[i]) for i in range(5)]
    then = [pltpu.make_async_copy(place[i], dst[i], out_sem.at[i // 4]) for i in range(5)]
    for copy in first:
        copy.start()
    for copy, onward in zip(first, then):
        copy.wait()
        onward.start()
    pltpu.make_async_copy(buf, buf, out_sem.at[0]).wait()
    then[4].wait()


def shards(q_proj, k_proj, v_proj, filt, skip, grad_out):
    n_ctx = lax.axis_size("ctx")
    scale = 1.0 / (16.0 * ROWS * n_ctx) ** 0.5
    hbm = pl.BlockSpec(memory_space=pltpu.HBM)
    big = jax.ShapeDtypeStruct((ROWS, LANES), BF16)
    results = (big, big, big, big, jax.ShapeDtypeStruct((4, 256), F32))
    pile = 2 * n_ctx // SHEET
    outs = pl.pallas_call(
        functools.partial(kernel, n_ctx, scale),
        out_shape=results,
        in_specs=[hbm] * 6,
        out_specs=(hbm,) * 5,
        scratch_shapes=[pltpu.VMEM((ROWS, LANES), BF16)] * 4
        + [
            pltpu.VMEM((TAPS, 128), F32),
            pltpu.VMEM((1, LANES), F32),
            pltpu.VMEM((3, TILES, ROWS, 128), BF16),
            pltpu.VMEM((3, TILES, ROWS, 128), BF16),
            pltpu.VMEM((2, TILES // 2, ROWS, 128), BF16),
            pltpu.VMEM((TILES, BLK, SLOTS * 128), BF16),
            pltpu.VMEM((TILES, ROWS, 256), F32),
            pltpu.VMEM((8, BLK, 128), BF16),
            pltpu.VMEM((4, 272, 128), F32),
            pltpu.VMEM((TILES, TAPS, 128), F32),
            pltpu.VMEM((4, 304, 128), F32),
            pltpu.VMEM((TAPS, 128), F32),
            pltpu.VMEM((SHEET, 2 * pile, 128), F32),
            pltpu.VMEM((SHEET, 2 * pile, 128), F32),
            pltpu.VMEM((pile // 2, 4, 128), F32),
            pltpu.VMEM((pile, 4, 128), F32),
        ]
        + [pltpu.VMEM((ROWS, LANES), BF16)] * 4
        + [
            pltpu.VMEM((4, 256), F32),
            pltpu.SemaphoreType.DMA((4, 3)),
            pltpu.SemaphoreType.DMA((4,)),
            pltpu.SemaphoreType.DMA((2,)),
            pltpu.SemaphoreType.DMA((2,)),
            pltpu.SemaphoreType.DMA((2, CHUNKS)),
            pltpu.SemaphoreType.DMA((2,)),
            pltpu.SemaphoreType.DMA((2, HALF)),
            pltpu.SemaphoreType.DMA((2,)),
            pltpu.SemaphoreType.DMA((2,)),
            pltpu.SemaphoreType.DMA,
            pltpu.SemaphoreType.DMA,
            pltpu.SemaphoreType.DMA,
            pltpu.SemaphoreType.DMA,
        ],
        compiler_params=pltpu.CompilerParams(
            collective_id=0, has_side_effects=True, vmem_limit_bytes=60 * 1024 * 1024
        ),
        cost_estimate=pl.CostEstimate(flops=3 * 10**9, bytes_accessed=4 * 2**20, transcendentals=0),
        name="hyena",
    )(q_proj, k_proj, v_proj, filt, skip.reshape(1, LANES), grad_out)
    outs = pl.pallas_call(
        hand_over,
        out_shape=results,
        in_specs=[hbm] * 5,
        out_specs=(hbm,) * 5,
        scratch_shapes=[
            pltpu.VMEM((4, ROWS, LANES), BF16),
            pltpu.VMEM((4, 256), F32),
            pltpu.SemaphoreType.DMA((5,)),
            pltpu.SemaphoreType.DMA((2,)),
        ],
        compiler_params=pltpu.CompilerParams(vmem_limit_bytes=60 * 1024 * 1024),
        cost_estimate=pl.CostEstimate(flops=0, bytes_accessed=4 * 2**20, transcendentals=0),
        name="hand_over",
    )(*outs)
    return tuple(outs)


def solution(mesh):
    in_specs = (
        P("ctx", "ch"),
        P("ctx", "ch"),
        P("ctx", "ch"),
        P(None, "ch"),
        P("ch"),
        P("ctx", "ch"),
    )
    out_specs = (P("ctx", "ch"), P("ctx", "ch"), P("ctx", "ch"), P("ctx", "ch"), P("ctx", None))
    return jax.shard_map(shards, mesh=mesh, in_specs=in_specs, out_specs=out_specs, check_vma=False)
```

```python
import functools

import jax
import jax.numpy as jnp
from jax import lax
from jax.experimental import pallas as pl
from jax.experimental.pallas import tpu as pltpu
from jax.sharding import PartitionSpec as P

MESH = pl.DeviceIdType.MESH
F32 = jnp.float32
BF16 = jnp.bfloat16
ROWS = 128
LANES = 2048
TILES = LANES // 128
CHUNKS = 8
HALF = CHUNKS // 2
SHEET = 16
PER = TILES // CHUNKS
WIDTH = PER * 128
BLK = 16
NB = ROWS // BLK
TAPS = 256
SPAN = TAPS // BLK + 1
SLOTS = SPAN + 2 * (NB - 1)


def iota(shape, dim):
    return lax.broadcasted_iota(jnp.int32, shape, dim)


def kernel(
    n_ctx, scale,
    q_hbm, k_hbm, v_hbm, filt_hbm, skip_hbm, g_hbm,
    mo_hbm, qg_hbm, kg_hbm, vg_hbm, fg_hbm,
    in_ref, filt_ref, skip_ref,
    x_ref, dc_ref, m_ref, s_ref, o_ref, mask_ref, sh_ref, z_ref, tsh_ref,
    d_ref, d1_ref, r1_ref, a1_ref, r2_ref,
    mo_ref, qg_ref, kg_ref, vg_ref, fg_ref,
    in_sem, out_sem, small_sem, far_send, far_recv, near_send, near_recv, mate_send, mate_recv,
    s1_send, s1_recv, s2_send, s2_recv,
):
    q_ref, k_ref, v_ref, g_ref = (in_ref.at[n] for n in range(4))
    d = lax.axis_index("ctx")
    h = lax.axis_index("ch")
    up = lax.rem(d + 2, n_ctx)
    down = lax.rem(d + n_ctx - 2, n_ctx)
    core = lax.rem(d, 2)
    mate = d + 1 - 2 * core
    layer = lax.div(d, 2 * SHEET)
    spot = lax.rem(lax.div(d, 2), SHEET)
    pile = 2 * n_ctx // SHEET
    e = (layer * 2 + core) * 2 + h

    def turn(n, p):
        return (lax.rem(p + HALF, CHUNKS) if not isinstance(p, int) else (p + HALF) % CHUNKS) if n == 0 else p

    def load(n, part):
        src, dst = ((k_hbm, k_ref), (v_hbm, v_ref), (g_hbm, g_ref), (q_hbm, q_ref))[n]
        first, count = ((0, 1), (1, HALF - 1), (HALF, HALF))[part]
        cols = pl.ds(turn(n // 2, first) * WIDTH, count * WIDTH)
        return pltpu.make_async_copy(src.at[:, cols], dst.at[:, cols], in_sem.at[part])


    def loaded(part):
        four = in_ref.at[:, :, pl.ds(0, (1, HALF - 1, HALF)[part] * WIDTH)]
        pltpu.make_async_copy(four, four, in_sem.at[part]).wait()

    def stage1_peer(step):
        other = lax.rem(spot + step, SHEET)
        return other, (layer * SHEET + other) * 2 + core, h

    def stage2_peer(step):
        other = lax.rem(e + step, pile)
        ctx = (lax.div(other, 4) * SHEET + spot) * 2 + lax.rem(lax.div(other, 2), 2)
        return other, ctx, lax.rem(other, 2)

    barrier = pltpu.get_barrier_semaphore()
    peers = [(up, h), (down, h)]
    peers += [stage1_peer(step)[1:] for step in range(1, SHEET)]
    peers += [stage2_peer(step)[1:] for step in range(1, pile)]
    for peer in peers:
        pl.semaphore_signal(barrier, inc=1, device_id=peer, device_id_type=MESH)
    for n in range(4):
        load(n, 0).start()
    for part in range(1, 3):
        for n in range(4):
            load(n, part).start()
    load_filt = pltpu.make_async_copy(filt_hbm, filt_ref, small_sem.at[0])
    load_skip = pltpu.make_async_copy(skip_hbm, skip_ref, small_sem.at[1])
    load_filt.start()
    load_skip.start()

    flip = (iota((ROWS, ROWS), 0) + iota((ROWS, ROWS), 1) == ROWS - 1).astype(F32).astype(BF16)
    fr, fc = iota((ROWS, 2 * ROWS), 0), iota((ROWS, 2 * ROWS), 1) % ROWS
    flip2 = (jnp.logical_and(fr // BLK == fc // BLK, fr % BLK + fc % BLK == BLK - 1)).astype(F32).astype(BF16)
    for g in range(8):
        mask_ref[g] = (iota((BLK, 128), 1) // BLK == g).astype(F32).astype(BF16)

    def far(n, c):
        ref, target = ((x_ref, up), (dc_ref, down))[n]
        cs = pl.ds(c * PER, PER)
        return pltpu.make_async_remote_copy(
            src_ref=ref.at[0, cs], dst_ref=ref.at[2, cs],
            send_sem=far_send.at[n], recv_sem=far_recv.at[n, c],
            device_id=(target, h), device_id_type=MESH,
        )

    def near(n, c, src_slot):
        ref = (x_ref, dc_ref)[n]
        cs = pl.ds(c * PER, PER)
        return pltpu.make_async_remote_copy(
            src_ref=ref.at[src_slot, cs], dst_ref=ref.at[1, cs],
            send_sem=near_send.at[n], recv_sem=near_recv.at[n, lax.rem(c, HALF)],
            device_id=(mate, h), device_id_type=MESH,
        )

    def gate(p):
        c0, c1 = turn(0, p), turn(1, p)
        if isinstance(p, int):
            loaded(0)
        else:
            for part, first in ((1, 1), (2, HALF)):

                @pl.when(p == first)
                def _():
                    loaded(part)

        cols = pl.ds(c0 * WIDTH if isinstance(p, int) else pl.multiple_of(c0 * WIDTH, WIDTH), WIDTH)
        st = (k_ref[:, cols].astype(F32) * v_ref[:, cols].astype(F32)).astype(BF16)
        st = jnp.dot(flip, st, preferred_element_type=F32).astype(BF16)
        for t in range(PER):
            x_ref[0, c0 * PER + t] = st[:, t * 128 : (t + 1) * 128]
        cols = pl.ds(c1 * WIDTH if isinstance(p, int) else pl.multiple_of(c1 * WIDTH, WIDTH), WIDTH)
        dc = (g_ref[:, cols].astype(F32) * q_ref[:, cols].astype(F32)).astype(BF16)
        for t in range(PER):
            dc_ref[0, c1 * PER + t] = dc[:, t * 128 : (t + 1) * 128]

    def to_mate(n, p):
        ref = (x_ref, dc_ref)[n]
        return pltpu.make_async_remote_copy(
            src_ref=ref.at[0, pl.ds(turn(n, p) * PER, PER)], dst_ref=m_ref.at[n, pl.ds((p - HALF) * PER, PER)],
            send_sem=mate_send.at[n], recv_sem=mate_recv.at[n],
            device_id=(mate, h), device_id_type=MESH,
        )

    def send(p):
        c0, c1 = turn(0, p), turn(1, p)
        far(0, c0).start()
        far(1, c1).start()
        if not isinstance(p, int):

            @pl.when(p >= HALF)
            def _():
                to_mate(0, p).start()
                to_mate(1, p).start()


        @pl.when(core == 0)
        def _():
            near(0, c0, 0).start()

        @pl.when(core == 1)
        def _():
            near(1, c1, 0).start()

    gate(0)
    pl.semaphore_wait(barrier, len(peers))
    send(0)
    def gate_step(p, carry):
        gate(p)
        send(p)
        return carry

    lax.fori_loop(1, CHUNKS, gate_step, 0)

    amt = 15 - iota((288, 128), 1) % BLK

    def table(c, carry):
        spots = iota((128, 512), 0) == 32 * c + iota((128, 512), 1) // BLK
        f = jnp.dot(filt_ref[...].astype(BF16), spots.astype(F32).astype(BF16), preferred_element_type=F32)
        edge = jnp.zeros((16, 128), F32)
        for t in range(4):
            z = jnp.concatenate([edge, f[:, t * 128 : (t + 1) * 128], edge], axis=0)
            for b in (8, 4, 2, 1):
                tsh_ref[t, 8:296] = z
                z = jnp.where((amt & b) != 0, tsh_ref[t, 8 - b : 296 - b], z)
            zb = z.astype(BF16)
            for u in range(SPAN):
                s_ref[c * 4 + t, :, (NB - 1 + u) * 128 : (NB + u) * 128] = zb[16 + 16 * u : 32 + 16 * u]
        return carry


    def spread(block):
        n_u = block.shape[0] // BLK
        wide = block.reshape(n_u, 1, BLK, 128) * mask_ref[...][None]
        return wide.reshape(n_u * 128, 128)

    def operator(n, u0, n_u):
        return jnp.concatenate(
            [s_ref[n, :, (NB - 1 - i + u0) * 128 : (NB - 1 - i + u0 + n_u) * 128] for i in range(NB)], axis=0
        )

    def own(c, carry):
        for t in range(4):
            n = c * 4 + t
            rhs = jnp.concatenate([spread(x_ref[0, n]), spread(dc_ref[0, n])], axis=1)
            o_ref[n] = jnp.dot(operator(n, 0, NB), rhs, preferred_element_type=F32)
        return carry

    amt2 = 15 - iota((264, 128), 1) % BLK
    even, odd = 1.0 - core.astype(F32), core.astype(F32)

    def filter_tiles(p):
        tiles = [(p * PER + t, dc_ref, x_ref, 0, even) for t in range(PER)]
        return tiles + [((p + HALF) * PER + t, x_ref, dc_ref, 1, odd) for t in range(PER)]

    def correlate(block, n, short, side):
        pad = jnp.zeros(((NB - 1) * BLK, 128), BF16)
        rows = jnp.concatenate([pad, block, pad], axis=0)
        lhs = jnp.concatenate([rows[BLK * i : BLK * i + (2 * NB - 1) * BLK] for i in range(NB)], axis=1)
        both = (spread(short[0, n]), spread(m_ref[side, n - side * HALF * PER]))
        rhs = [jnp.concatenate([b[(NB - 1 - i) * 128 : (NB - i) * 128] for i in range(NB)], axis=1) for b in both]
        rhs = jnp.concatenate(rhs, axis=0)
        return lax.dot_general(lhs, rhs, (((1,), (1,)), ((), ())), preferred_element_type=F32)

    def filter_near(p):
        for n, long, short, side, far_weight in filter_tiles(p):
            y = correlate(long[0, n], n, short, side)
            z_ref[n, 0:16] = y[112:128, :128]
            z_ref[n, 16:128] = y[128:240, :128] + (1.0 - far_weight) * y[0:112, 128:]
            z_ref[n, 128:256] = (1.0 - far_weight) * y[112:240, 128:]

    def filter_terms(p):
        tiles = filter_tiles(p)
        parts, spots = [], []
        for t, (n, long, short, side, far_weight) in enumerate(tiles):
            y = correlate(long[2, n], n, short, side)
            sh_ref[t, 0:16] = z_ref[n, 0:16]
            sh_ref[t, 16:144] = z_ref[n, 16:144] + far_weight * y[0:128, 128:]
            sh_ref[t, 144:256] = z_ref[n, 144:256] + far_weight * y[128:240, 128:] + y[0:112, :128]
            sh_ref[t, 256:272] = y[112:128, :128]
        for t, (n, long, short, side, far_weight) in enumerate(tiles):
            z = jnp.where((amt2 & 8) != 0, sh_ref[t, 8:272], sh_ref[t, 0:264])
            for b in (4, 2, 1):
                sh_ref[t, 0:264] = z
                z = jnp.where((amt2 & b) != 0, sh_ref[t, b : 264 + b], z)
            z = z[:TAPS]
            hi = z.astype(BF16)
            parts += [hi, (z - hi.astype(F32)).astype(BF16)]
            spot = (iota((256, 128), 1) == 8 * n + iota((256, 128), 0) % 128 // BLK).astype(F32)
            spots.append(spot.astype(BF16))
        terms = jnp.dot(
            jnp.concatenate(parts, axis=1), jnp.concatenate(spots, axis=0), preferred_element_type=F32
        )
        d_ref[...] += terms

    def store(n, c):
        src, dst = ((mo_ref, mo_hbm), (qg_ref, qg_hbm), (kg_ref, kg_hbm), (vg_ref, vg_hbm))[n]
        cols = pl.ds(c * WIDTH if isinstance(c, int) else pl.multiple_of(c * WIDTH, WIDTH), WIDTH)
        return pltpu.make_async_copy(src.at[:, cols], dst.at[:, cols], out_sem.at[n])

    def rest(p):
        tiles = [p * PER + t for t in range(PER)] + [(p + HALF) * PER + t for t in range(PER)]
        his, los = [], []
        for n in tiles:
            rx = jnp.concatenate([spread(x_ref[1, n]), spread(x_ref[2, n])], axis=0)
            rd = jnp.concatenate([spread(dc_ref[1, n]), spread(dc_ref[2, n])], axis=0)
            out = o_ref[n] + jnp.dot(
                operator(n, NB, 2 * NB), jnp.concatenate([rx, rd], axis=1), preferred_element_type=F32
            )
            o_ref[n] = out
            ds = out[:, 128:]
            hi = ds.astype(BF16)
            his.append(hi)
            los.append((ds - hi.astype(F32)).astype(BF16))
        pair = jnp.concatenate([jnp.concatenate(his, axis=1), jnp.concatenate(los, axis=1)], axis=0)
        flipped = jnp.dot(flip2, pair, preferred_element_type=F32)
        for t, n in enumerate(tiles):
            ls = pl.ds(n * 128 if isinstance(n, int) else pl.multiple_of(n * 128, 128), 128)
            conv = jnp.concatenate(
                [o_ref[n, BLK * (NB - 1 - i) : BLK * (NB - i), :128] for i in range(NB)], axis=0
            )
            ds = flipped[:, t * 128 : (t + 1) * 128]
            kf, vf = k_ref[:, ls].astype(F32), v_ref[:, ls].astype(F32)
            qf, gf = q_ref[:, ls].astype(F32), g_ref[:, ls].astype(F32)
            skip = skip_ref[:, ls]
            conv = conv + skip * (kf * vf).astype(BF16).astype(F32)
            ds = ds + skip * dc_ref[0, n].astype(F32)
            mo_ref[:, ls] = (qf * conv).astype(BF16)
            qg_ref[:, ls] = (gf * conv).astype(BF16)
            kg_ref[:, ls] = (ds * vf).astype(BF16)
            vg_ref[:, ls] = (ds * kf).astype(BF16)
        for c in (p, p + HALF):
            for n in range(4):
                store(n, c).start()

    def arrive(p):
        c0, c1 = turn(0, p), turn(1, p)
        far(0, c0).wait_recv()

        @pl.when(d < 2)
        def _():
            x_ref[2, pl.ds(c0 * PER, PER)] = jnp.zeros((PER, ROWS, 128), BF16)

        @pl.when(core == 1)
        def _():
            near(0, c0, 2).start()

        far(1, c1).wait_recv()

        @pl.when(d >= n_ctx - 2)
        def _():
            dc_ref[2, pl.ds(c1 * PER, PER)] = jnp.zeros((PER, ROWS, 128), BF16)

        @pl.when(core == 0)
        def _():
            near(1, c1, 2).start()

    def complete(p):
        for n in range(2):
            two = (x_ref, dc_ref)[n].at[1, pl.ds(0, 2 * PER)]
            pltpu.make_async_copy(two, two, near_recv.at[n, p]).wait()

    def stage1(step):
        other, ctx, ch = stage1_peer(step)
        return pltpu.make_async_remote_copy(
            src_ref=d1_ref.at[other], dst_ref=r1_ref.at[spot],
            send_sem=s1_send, recv_sem=s1_recv,
            device_id=(ctx, ch), device_id_type=MESH,
        )

    def stage2(step):
        other, ctx, ch = stage2_peer(step)
        return pltpu.make_async_remote_copy(
            src_ref=a1_ref.at[lax.div(other, 2)], dst_ref=r2_ref.at[e],
            send_sem=s2_send, recv_sem=s2_recv,
            device_id=(ctx, ch), device_id_type=MESH,
        )

    for n in range(2):
        pltpu.make_async_copy(m_ref.at[n], m_ref.at[n], mate_recv.at[n]).wait()
    def near_step(p, carry):
        filter_near(p)
        return carry

    def far_step(p, carry):
        arrive(p)
        filter_terms(p)
        return carry

    d_ref[...] = jnp.zeros_like(d_ref)
    lax.fori_loop(0, HALF, near_step, 0)
    lax.fori_loop(0, HALF, far_step, 0)
    for n in range(SHEET):
        rows = [d_ref[pl.ds(z * 8 * SHEET + 8 * n, 8)] for z in range(pile // 4)]
        d1_ref[n] = jnp.concatenate(rows, axis=0)
    for step in range(1, SHEET):
        stage1(step).start()
    load_filt.wait()
    load_skip.wait()
    s_ref[:, :, : (NB - 1) * 128] = jnp.zeros((TILES, BLK, (NB - 1) * 128), BF16)
    s_ref[:, :, (NB - 1 + SPAN) * 128 :] = jnp.zeros((TILES, BLK, (NB - 1) * 128), BF16)
    tsh_ref[...] = jnp.zeros_like(tsh_ref)
    lax.fori_loop(0, TILES // 4, table, 0)
    arrive(4)
    lax.fori_loop(0, TILES // 4, own, 0)
    arrive(5)
    complete(0)
    rest(0)
    total = jnp.concatenate([d_ref[pl.ds(z * 8 * SHEET + 8 * spot, 8)] for z in range(pile // 4)], axis=0)
    others = r1_ref.at[pl.ds(0, SHEET - 1)]
    pltpu.make_async_copy(others, others, s1_recv).wait()
    for step in range(1, SHEET):
        total = total + r1_ref[stage1_peer(step)[0]]
    total = total * scale
    for n in range(pile // 2):
        a1_ref[n] = total[4 * n : 4 * n + 4]
    r2_ref[e] = a1_ref[lax.div(e, 2)]
    for step in range(1, pile):
        stage2(step).start()

    def rest_step(p, carry):
        @pl.when(p + 1 < HALF)
        def _():
            arrive(p + HALF + 1)

        complete(p)
        rest(p)
        return carry

    lax.fori_loop(1, HALF, rest_step, 0)
    rest_of_pile = r2_ref.at[pl.ds(0, pile - 1)]
    pltpu.make_async_copy(rest_of_pile, rest_of_pile, s2_recv).wait()
    for hh in range(2):
        total = r2_ref[hh]
        for n in range(1, pile // 2):
            total = total + r2_ref[n * 2 + hh]
        fg_ref[:, hh * 128 : (hh + 1) * 128] = total

    last = pltpu.make_async_copy(fg_ref, fg_hbm, small_sem.at[0])
    last.start()

    for n, (src, dst) in enumerate(((mo_ref, mo_hbm), (qg_ref, qg_hbm), (kg_ref, kg_hbm), (vg_ref, vg_hbm))):
        pltpu.make_async_copy(src, dst, out_sem.at[n]).wait()
    for n in range(2):
        whole = (x_ref, dc_ref)[n].at[0]
        pltpu.make_async_copy(whole, whole, far_send.at[n]).wait()
        pltpu.make_async_copy(whole, whole, near_send.at[n]).wait()
        pltpu.make_async_copy(m_ref.at[n], m_ref.at[n], mate_send.at[n]).wait()
    pltpu.make_async_copy(others, others, s1_send).wait()
    pltpu.make_async_copy(rest_of_pile, rest_of_pile, s2_send).wait()
    last.wait()


def hand_over(*refs):
    src, dst, buf, small = refs[:5], refs[5:10], refs[10], refs[11]
    in_sem, out_sem = refs[12:]
    place = [buf.at[i] for i in range(4)] + [small]
    first = [pltpu.make_async_copy(src[i], place[i], in_sem.at[i]) for i in range(5)]
    then = [pltpu.make_async_copy(place[i], dst[i], out_sem.at[i // 4]) for i in range(5)]
    for copy in first:
        copy.start()
    for copy, onward in zip(first, then):
        copy.wait()
        onward.start()
    pltpu.make_async_copy(buf, buf, out_sem.at[0]).wait()
    then[4].wait()


def shards(q_proj, k_proj, v_proj, filt, skip, grad_out):
    n_ctx = lax.axis_size("ctx")
    scale = 1.0 / (16.0 * ROWS * n_ctx) ** 0.5
    hbm = pl.BlockSpec(memory_space=pltpu.HBM)
    big = jax.ShapeDtypeStruct((ROWS, LANES), BF16)
    results = (big, big, big, big, jax.ShapeDtypeStruct((4, 256), F32))
    pile = 2 * n_ctx // SHEET
    outs = pl.pallas_call(
        functools.partial(kernel, n_ctx, scale),
        out_shape=results,
        in_specs=[hbm] * 6,
        out_specs=(hbm,) * 5,
        scratch_shapes=[
            pltpu.VMEM((4, ROWS, LANES), BF16),
            pltpu.VMEM((TAPS, 128), F32),
            pltpu.VMEM((1, LANES), F32),
            pltpu.VMEM((3, TILES, ROWS, 128), BF16),
            pltpu.VMEM((3, TILES, ROWS, 128), BF16),
            pltpu.VMEM((2, TILES // 2, ROWS, 128), BF16),
            pltpu.VMEM((TILES, BLK, SLOTS * 128), BF16),
            pltpu.VMEM((TILES, ROWS, 256), F32),
            pltpu.VMEM((8, BLK, 128), BF16),
            pltpu.VMEM((4, 272, 128), F32),
            pltpu.VMEM((TILES, TAPS, 128), F32),
            pltpu.VMEM((4, 304, 128), F32),
            pltpu.VMEM((TAPS, 128), F32),
            pltpu.VMEM((SHEET, 2 * pile, 128), F32),
            pltpu.VMEM((SHEET, 2 * pile, 128), F32),
            pltpu.VMEM((pile // 2, 4, 128), F32),
            pltpu.VMEM((pile, 4, 128), F32),
        ]
        + [pltpu.VMEM((ROWS, LANES), BF16)] * 4
        + [
            pltpu.VMEM((4, 256), F32),
            pltpu.SemaphoreType.DMA((3,)),
            pltpu.SemaphoreType.DMA((4,)),
            pltpu.SemaphoreType.DMA((2,)),
            pltpu.SemaphoreType.DMA((2,)),
            pltpu.SemaphoreType.DMA((2, CHUNKS)),
            pltpu.SemaphoreType.DMA((2,)),
            pltpu.SemaphoreType.DMA((2, HALF)),
            pltpu.SemaphoreType.DMA((2,)),
            pltpu.SemaphoreType.DMA((2,)),
            pltpu.SemaphoreType.DMA,
            pltpu.SemaphoreType.DMA,
            pltpu.SemaphoreType.DMA,
            pltpu.SemaphoreType.DMA,
        ],
        compiler_params=pltpu.CompilerParams(
            collective_id=0, has_side_effects=True, vmem_limit_bytes=60 * 1024 * 1024
        ),
        cost_estimate=pl.CostEstimate(flops=3 * 10**9, bytes_accessed=4 * 2**20, transcendentals=0),
        name="hyena",
    )(q_proj, k_proj, v_proj, filt, skip.reshape(1, LANES), grad_out)
    outs = pl.pallas_call(
        hand_over,
        out_shape=results,
        in_specs=[hbm] * 5,
        out_specs=(hbm,) * 5,
        scratch_shapes=[
            pltpu.VMEM((4, ROWS, LANES), BF16),
            pltpu.VMEM((4, 256), F32),
            pltpu.SemaphoreType.DMA((5,)),
            pltpu.SemaphoreType.DMA((2,)),
        ],
        compiler_params=pltpu.CompilerParams(vmem_limit_bytes=60 * 1024 * 1024),
        cost_estimate=pl.CostEstimate(flops=0, bytes_accessed=4 * 2**20, transcendentals=0),
        name="hand_over",
    )(*outs)
    return tuple(outs)


def solution(mesh):
    in_specs = (
        P("ctx", "ch"),
        P("ctx", "ch"),
        P("ctx", "ch"),
        P(None, "ch"),
        P("ch"),
        P("ctx", "ch"),
    )
    out_specs = (P("ctx", "ch"), P("ctx", "ch"), P("ctx", "ch"), P("ctx", "ch"), P("ctx", None))
    return jax.shard_map(shards, mesh=mesh, in_specs=in_specs, out_specs=out_specs, check_vma=False)
```
